512 devices in a mesh: tok: 16 (over y, x), col: 32 (over z, core).
Axes of the slice: x: 4, y: 4, z: 16, core: 2. Of those that a mesh axis runs over, the one named last changes fastest.
Arguments:
- rollout: bfloat16 [2048, 5120], P('tok'), may hold values from -6 to 6
- lengths: int32 [32], P('tok'), may hold values from 16 to 64
- route: int32 [2048, 1], P('tok'), may hold values from 0 to 15; in each aligned block of 128 rows (0 to 127, 128 to 255, ...) at most 16 rows name the same one
- up_codes: bfloat16 [5120, 16384], P('tok', 'col'), may hold values from -4 to 4
- up_scales: float32 [20, 64], P(None, 'col'), may hold values from 0.0069877123 to 0.02795085
- block_rows: int32 [64, 2], P('col'), may hold values from 0 to 19, as said below
- delta: float32 [256, 64, 2, 256], P('tok', 'col'), may hold values from -0.125 to 0.125
- adam_m: float32 [256, 64, 2, 256], P('tok', 'col'), may hold values from -12 to 12
- adam_v: float32 [256, 64, 2, 256], P('tok', 'col'), may hold values from 1 to 30
- gate_pre: bfloat16 [4096, 16384], P('tok', 'col'), may hold values from -8 to 8
- hidden_grad: bfloat16 [4096, 16384], P('tok', 'col'), may hold values from -0.875 to 0.875
Outputs:
- input_grad: bfloat16 [4096, 5120], P('tok', 'col')
- gate_grad: bfloat16 [4096, 16384], P('tok', 'col')
- new_delta: float32 [256, 64, 2, 256], P('tok', 'col')
- new_m: float32 [256, 64, 2, 256], P('tok', 'col')
- new_v: float32 [256, 64, 2, 256], P('tok', 'col')
- delta_scale: float32 [64, 2], P('col')
- delta_codes: bfloat16 [256, 64, 2, 256], P('tok', 'col')
The draws below stay inside these ranges and needn't reach their ends.
Inputs may be any that keep to these rules, and one draw needn't show every extreme that they name: `route`: at most 16 of the 128 rows of one index of tok name the same learner shard, and some learner shard is named by exactly 16 of them. `block_rows`: the 2 row blocks of one column block are distinct.
All inputs are finite; a program needn't handle non-finite values. Where the reference program divides by a largest or mean magnitude, that divisor is 1e-20 or more.
Results may differ from the reference program's by a relative error of at most 0.017.
Values may be sent and summed in bfloat16 or wider, within the bound.
A program may use at most 128 MiB of HBM per device.

```python
import math
import jax
import jax.numpy as jnp
import numpy as np
from jax import lax

D = 5120
BLK = 256
K = 2
RESP = 64
STEP = 1000
TOK_DEV = 128
SEND = 2048
SEQS = 32
CAP = 16
LROWS = 256
LEARN = 4096
FFB = 64
FF = 16384
DB = 20
N_TOK = 16
N_COL = 32


def draw_block_rows(key, part):
    key = jax.random.fold_in(key, 7)
    scores = jax.random.randint(key, (FFB, DB), 0, 65536) * DB + jnp.arange(DB, dtype=jnp.int32)[None, :]
    return lax.top_k(scores, K)[1].astype(jnp.int32)


def place_ends(result, rng, smallest, top_value):
    spot = [jax.random.randint(jax.random.fold_in(rng, axis), (), 0, length) for axis, length in enumerate(result.shape)]
    longest = result.shape.index(max(result.shape))
    next_to = spot[:longest] + [(spot[longest] + 1) % result.shape[longest]] + spot[longest + 1:]
    return result.at[tuple(spot)].set(smallest).at[tuple(next_to)].set(top_value)


def steps_of(stream_key, dims, cuts, low, top_value):
    def one(dim, shards_of):
        draws = jax.random.uniform(jax.random.fold_in(jax.random.fold_in(stream_key, 6), dim), (shards_of,), jnp.float32, low / len(cuts), top_value / len(cuts))
        return jnp.repeat(jnp.exp(draws), dims[dim] // shards_of).reshape((-1,) + (1,) * (len(dims) - dim - 1))

    factor_of = one(*cuts[0])
    for cut in cuts[1:]:
        factor_of = factor_of * one(*cut)
    return factor_of


def assign_block(stream_key, own, number, rows, number_of, top, bound, skew):
    sequence = jax.random.permutation(stream_key, number_of)
    heavy_load, ordinary = portions_of(number_of, rows * top, bound, skew, True), portions_of(number_of, rows * top, bound, skew, False)
    places = jnp.arange(number_of)

    def named(sizes, offset_by):
        used = int((sizes > 0).sum())
        fixed = max(1, used // 4)
        moved = fixed + (places - fixed + offset_by * (used - fixed)) % max(1, number_of - fixed)
        return jnp.zeros((number_of,), jnp.int32).at[sequence[jnp.where(places < fixed, places, moved)]].set(jnp.asarray(sizes, jnp.int32))

    sizes = jnp.where(number % 4 == 0, named(heavy_load, number // 4), named(ordinary, number - number // 4 - 1))
    mixed = jax.random.permutation(jax.random.fold_in(own, 3), number_of)
    giver, receiver = mixed[0:number_of // 2 * 2:2], mixed[1:number_of // 2 * 2:2]
    margin = jnp.minimum(sizes[giver] - 1, bound - sizes[receiver]) // 2
    margin = jnp.where((giver == sequence[0]) | (receiver == sequence[0]) | (sizes[receiver] == 0), 0, jnp.maximum(margin, 0))
    moved = jax.random.randint(jax.random.fold_in(own, 4), (number_of // 2,), 0, 1 << 20) % (margin + 1)
    sizes = sizes.at[giver].add(-moved).at[receiver].add(moved)
    items = jnp.searchsorted(jnp.cumsum(sizes), jnp.arange(rows * top), side="right").astype(jnp.int32)
    listing = items.reshape(top, rows).T
    listing = listing[jax.random.permutation(jax.random.fold_in(own, 1), rows)]
    offset_by = jax.random.randint(jax.random.fold_in(own, 2), (rows, 1), 0, top)
    return jnp.take_along_axis(listing, (jnp.arange(top)[None, :] + offset_by) % top, axis=1)


def portions_of(amount, total, most, lean, full):
    portions = [(1 << 20) // math.isqrt(standing ** lean) + 1 for standing in range(1, amount + 1)]
    largest = most if full else min(most, max(-(-total // amount), total * portions[0] // sum(portions)))
    least = 1 if total - largest >= amount - 1 else 0
    given, spare = [largest] + [least] * (amount - 1), total - largest - least * (amount - 1)
    while spare > 0:
        candidates = [i for i in range(1, amount) if given[i] < largest] or [i for i in range(1, amount) if given[i] < most]
        whole, remaining = sum([portions[i] for i in candidates]), spare
        for i in candidates:
            addition = min(most - given[i], max(1, remaining * portions[i] // whole), spare)
            given[i] = given[i] + addition
            spare = spare - addition
    return np.array(given)


def scatter_about(stream_key, dims, scale, bound, shards=(), kind=jnp.bfloat16):
    array = jax.random.normal(stream_key, dims, jnp.float32) * scale
    if len(shards) > 0:
        array = steps_of(stream_key, dims, shards, -0.22, 0.18) * array
    return jnp.clip(array, min=-bound, max=bound).astype(kind)


def setup_inputs(seed: int = 0) -> dict:
    splits = jax.random.split(jax.random.key(seed), 12)
    rollout = scatter_about(splits[0], (SEND, D), 1.0, 6.0, ((0, 16),))
    lengths = place_ends(jax.random.randint(splits[1], (SEQS,), RESP // 4, RESP + 1), jax.random.fold_in(splits[1], 1), RESP // 4, RESP).astype(jnp.int32)
    route_keys = jax.random.split(jax.random.fold_in(splits[2], 1), SEND // TOK_DEV)
    route_turns = jax.random.permutation(jax.random.fold_in(splits[2], 3), SEND // TOK_DEV)
    route = jax.vmap(lambda own, number: assign_block(jax.random.fold_in(splits[2], 2), own, number, TOK_DEV, N_TOK, 1, CAP, 2))(route_keys, route_turns).reshape((SEND, 1))
    up_codes = scatter_about(splits[3], (D, FF), 1.0, 4.0, ((0, 16), (1, 32)))
    up_scales = jnp.clip(jnp.exp(math.log(0.02795085) - 1.3862944 * jax.random.uniform(splits[4], (DB, FFB), jnp.float32) ** steps_of(splits[4], (DB, FFB), ((1, 32),), -0.2, 0.2)), 0.0069877123, 0.02795085)
    block_rows = draw_block_rows(jax.random.fold_in(splits[11], 71), 0)
    delta = scatter_about(splits[6], (BLK, FFB, K, BLK), (0.5 * (K * BLK) ** -0.5), 0.125, ((0, 16), (1, 32)), jnp.float32)
    adam_m = scatter_about(splits[7], (BLK, FFB, K, BLK), 2.0, 12.0, ((0, 16), (1, 32)), jnp.float32)
    adam_v = jnp.clip(jnp.exp(math.log(30.0) - 3.4011974 * jax.random.uniform(splits[8], (BLK, FFB, K, BLK), jnp.float32) ** steps_of(splits[8], (BLK, FFB, K, BLK), ((0, 16), (1, 32)), -0.2, 0.2)), 1.0, 30.0)
    gate_pre = scatter_about(splits[9], (LEARN, FF), 1.5, 8.0, ((0, 16), (1, 32)))
    hidden_grad = scatter_about(splits[10], (LEARN, FF), 0.15, 0.875, ((0, 16), (1, 32)))
    return dict(rollout=rollout, lengths=lengths, route=route, up_codes=up_codes, up_scales=up_scales, block_rows=block_rows, delta=delta, adam_m=adam_m, adam_v=adam_v, gate_pre=gate_pre, hidden_grad=hidden_grad)


beta_first = 0.9
beta_second = 0.999
step_rate = 0.01
adam_eps = 1e-08
scale_eps = 1e-06

def silu_slope(operand):
    sigmoid_value = jax.nn.sigmoid(operand)
    return sigmoid_value * (1.0 + operand * (1.0 - sigmoid_value))

def reference(rollout, lengths, route, up_codes, up_scales, block_rows, delta, adam_m, adam_v, gate_pre, hidden_grad):
    row_ids = jnp.arange(SEND, dtype=jnp.int32)
    seq_len = jnp.repeat(lengths, RESP)
    position = row_ids % RESP
    row_weight = jnp.where(position < seq_len, RESP / seq_len.astype(jnp.float32), 0.0).astype(jnp.float32)
    destination = route[:, 0]
    onehot = (destination[:, None] == jnp.arange(N_TOK, dtype=jnp.int32)[None, :]).astype(jnp.int32)
    ranks = jnp.cumsum(onehot.reshape(N_TOK, TOK_DEV, N_TOK), axis=1).reshape(SEND, N_TOK) - 1
    slot_index = lax.optimization_barrier(jnp.sum(ranks * onehot, axis=1)).astype(jnp.int32)
    target = (destination * LROWS + row_ids // TOK_DEV * CAP + slot_index).astype(jnp.int32)
    learn_x = jnp.zeros((LEARN, D), jnp.bfloat16).at[target].set(rollout)
    learn_w = jnp.zeros((LEARN,), jnp.float32).at[target].set(row_weight)
    scale_full = jnp.repeat(jnp.repeat(up_scales, BLK, axis=0), BLK, axis=1)
    up_weight = (up_codes.astype(jnp.float32) * scale_full).astype(jnp.bfloat16)
    delta_half = delta.astype(jnp.bfloat16)
    chosen = jnp.take(learn_x.reshape(LEARN, DB, BLK), block_rows.reshape(-1), axis=1).reshape(LEARN, FFB, K, BLK)
    activation = jax.nn.silu(gate_pre.astype(jnp.float32))
    up_grad = (hidden_grad.astype(jnp.float32) * activation * learn_w[:, None]).astype(jnp.bfloat16)
    up_grad_blocks = up_grad.reshape(LEARN, FFB, BLK)
    delta_up = jnp.einsum('rjkb,bjkc->rjc', chosen.astype(jnp.float32), delta_half.astype(jnp.float32)).reshape(LEARN, FF)
    up_value = jnp.dot(learn_x, up_weight, preferred_element_type=jnp.float32) + delta_up
    gate_grad = (hidden_grad.astype(jnp.float32) * up_value * silu_slope(gate_pre.astype(jnp.float32)) * learn_w[:, None]).astype(jnp.bfloat16)
    delta_back = jnp.einsum('rjc,bjkc->rjkb', up_grad_blocks.astype(jnp.float32), delta_half.astype(jnp.float32))
    group_blocks = FFB // N_COL
    group_width = FF // N_COL

    def add_group(summed, group_index):
        first_column = group_index * group_width
        grad_part = lax.dynamic_slice_in_dim(up_grad, first_column, group_width, 1)
        weight_part = lax.dynamic_slice_in_dim(up_weight, first_column, group_width, 1)
        partial_sum = lax.dot_general(grad_part, weight_part, (((1,), (1,)), ((), ())), preferred_element_type=jnp.float32)
        back_part = lax.dynamic_slice_in_dim(delta_back, group_index * group_blocks, group_blocks, 1).reshape(LEARN, group_blocks * K, BLK)
        rows_part = lax.dynamic_slice_in_dim(block_rows, group_index * group_blocks, group_blocks, 0).reshape(-1)
        placed = jnp.zeros((LEARN, DB, BLK), jnp.float32).at[:, rows_part].add(back_part)
        partial_sum = partial_sum + placed.reshape(LEARN, D)
        return (summed + partial_sum, None)
    summed = lax.scan(add_group, jnp.zeros((LEARN, D), jnp.float32), jnp.arange(N_COL, dtype=jnp.int32))[0]
    input_grad = summed.astype(jnp.bfloat16)
    gradient = jnp.einsum('rjkb,rjc->bjkc', chosen.astype(jnp.float32), up_grad_blocks.astype(jnp.float32))
    new_m = beta_first * adam_m + (1.0 - beta_first) * gradient
    new_v = beta_second * adam_v + (1.0 - beta_second) * gradient * gradient
    corrected_m = new_m / (1.0 - beta_first ** STEP)
    corrected_v = new_v / (1.0 - beta_second ** STEP)
    new_delta = delta - step_rate * corrected_m / (jnp.sqrt(corrected_v) + adam_eps)
    delta_scale = lax.optimization_barrier(jnp.max(jnp.abs(new_delta), axis=(0, 3)))
    delta_codes = (new_delta / (delta_scale + scale_eps)[None, :, :, None]).astype(jnp.bfloat16)
    return (input_grad, gate_grad, new_delta, new_m, new_v, delta_scale, delta_codes)
```

```python
import functools

import jax
import jax.numpy as jnp
from jax import lax
from jax.experimental import pallas as pl
from jax.experimental.pallas import tpu as pltpu
from jax.sharding import PartitionSpec as P

BLK = 256
RESP = 64
STEP = 1000
D = 5120
NT = 16
NZ = 16
CAP = 16
ROWS = 128
COLS = 512
KS = D // 4
CROWS = 320
DCH = KS // NZ
GB = 144

beta_first = 0.9
beta_second = 0.999
step_rate = 0.01
adam_eps = 1e-08
scale_eps = 1e-06

MESH = pl.DeviceIdType.MESH
F32 = jnp.float32
BF16 = jnp.bfloat16


def dot_nn(a, b):
    return lax.dot_general(a, b, (((1,), (0,)), ((), ())), preferred_element_type=F32)


def dot_nt(a, b):
    return lax.dot_general(a, b, (((1,), (1,)), ((), ())), preferred_element_type=F32)


def dot_tn(a, b):
    return lax.dot_general(a, b, (((0,), (0,)), ((), ())), preferred_element_type=F32)


def is_same(a, b):
    return (1 - jnp.minimum(jnp.abs(a - b), 1)).astype(F32)


class Links:
    def __init__(self, send, recv):
        self.send, self.recv = send, recv
        self.sent = []

    def copy(self, src, dst, number, tok, col):
        return pltpu.make_async_remote_copy(
            src_ref=src,
            dst_ref=dst,
            send_sem=self.send.at[number],
            recv_sem=self.recv.at[number],
            device_id={"tok": tok, "col": col},
            device_id_type=MESH,
        )

    def start(self, src, dst, number, tok, col):
        made = self.copy(src, dst, number, tok, col)
        made.start()
        self.sent.append(made)

    def wait(self, dst, number):
        pltpu.make_async_copy(dst, dst, self.recv.at[number]).wait()

    def drain(self):
        for made in self.sent:
            made.wait_send()


class RingGather:
    def __init__(self, links, me, device, block, half):
        self.links, self.block, self.half, self.device = links, block, half, device
        self.me = me
        self.right, self.left, self.far = (me + 1) % 4, (me + 3) % 4, (me + 2) % 4

    def put(self, src, index, part, number, to):
        self.links.start(self.half(src, part), self.half(self.block(index), part), number, *self.device(to))

    def got(self, index, part, number):
        self.links.wait(self.half(self.block(index), part), number)

    def begin(self, src):
        self.put(src, self.me, 0, 0, self.right)
        self.put(src, self.me, 1, 1, self.left)
        self.put(src, self.me, 1, 2, self.right)
        self.put(src, self.me, 0, 3, self.left)

    def forward(self):
        self.got(self.left, 0, 0)
        self.put(self.block(self.left), self.left, 0, 4, self.right)
        self.got(self.right, 1, 1)
        self.put(self.block(self.right), self.right, 1, 5, self.left)

    def finish(self):
        self.got(self.left, 1, 2)
        self.got(self.right, 0, 3)
        self.got(self.far, 0, 4)
        self.got(self.far, 1, 5)


class RingReduce:
    def __init__(self, links, me, device, part, half, first, stage, second):
        self.links, self.part, self.half, self.device = links, part, half, device
        self.first, self.stage, self.second = first, stage, second
        self.me = me
        self.right, self.left, self.far = (me + 1) % 4, (me + 3) % 4, (me + 2) % 4

    def put(self, src, dst, number, to):
        self.links.start(src, dst, number, *self.device(to))

    def begin(self):
        self.put(self.half(self.part(self.far), 0), self.first.at[0], 0, self.right)
        self.put(self.half(self.part(self.far), 1), self.first.at[1], 1, self.left)
        self.put(self.half(self.part(self.right), 1), self.half(self.second.at[0], 1), 2, self.right)
        self.put(self.half(self.part(self.left), 0), self.half(self.second.at[1], 0), 3, self.left)

    def forward(self):
        self.links.wait(self.first.at[0], 0)
        self.stage[0] = (
            self.half(self.part(self.right), 0)[...].astype(F32) + self.first[0].astype(F32)
        ).astype(BF16)
        self.put(self.stage.at[0], self.half(self.second.at[0], 0), 4, self.right)
        self.links.wait(self.first.at[1], 1)
        self.stage[1] = (
            self.half(self.part(self.left), 1)[...].astype(F32) + self.first[1].astype(F32)
        ).astype(BF16)
        self.put(self.stage.at[1], self.half(self.second.at[1], 1), 5, self.left)

    def finish(self):
        self.links.wait(self.half(self.second.at[0], 1), 2)
        self.links.wait(self.half(self.second.at[1], 0), 3)
        self.links.wait(self.half(self.second.at[0], 0), 4)
        self.links.wait(self.half(self.second.at[1], 1), 5)

    def total(self, own):
        return own + (self.second[0].astype(F32) + self.second[1].astype(F32))


def rows_half(size):
    def half(ref, part):
        return ref.at[pl.ds(part * size, size), :]

    return half


def lanes_half(size):
    def half(ref, part):
        return ref.at[:, pl.ds(part * size, size)]

    return half


def g_half(ref, part):
    return ref.at[pl.ds(0, 64), :] if part == 0 else ref.at[pl.ds(64, GB - 64), :]


def kernel(
    lengths, scales, brows, rollout, route, codes, delta, adam_m, adam_v, gate_pre, hidden_grad,
    ig_out, gg_out, nd_out, nm_out, nv_out, ds_out, dc_out,
    u_send, u_buf, slope, w_buf, w_eff, x_buf, d_buf, g_buf, g_all,
    h_part, h_first, h_stage, h_second, hs_send, hs_buf,
    q_part, q_first, q_stage, q_second, r_part, r_first, r_stage, r_second,
    m_send, m_buf, z_own, z_give, z_take, z_send, z_recv, f_send, f_buf, chosen_rows,
    c_ss, c_rs, dy_ss, dy_rs, dx_ss, dx_rs, g_ss, g_rs, x_ss, x_rs, h_ss, h_rs,
    q_ss, q_rs, r_ss, r_rs, s_ss, s_rs, z_ss, z_rs, a_ss, a_rs,
):
    t = lax.axis_index("tok")
    c = lax.axis_index("col")
    y, x = t // 4, t % 4
    z, h = c // 2, c % 2

    def at_x(other):
        return y * 4 + other, c

    def at_y(other):
        return other * 4 + x, c

    codes_ring = RingGather(
        Links(c_ss, c_rs), x, at_x, lambda i: w_buf.at[pl.ds(i * CROWS, CROWS), :], rows_half(CROWS // 2)
    )
    codes_ring.begin(codes)
    w_buf[pl.ds(x * CROWS, CROWS), :] = codes[...]

    x_links = Links(x_ss, x_rs)
    for step in (1, 3, 2):
        to = (y + step) % 4
        x_links.start(
            rollout.at[pl.ds(64 * h, 64), pl.ds(pl.multiple_of(to * KS, KS), KS)],
            x_buf.at[pl.ds(y * ROWS + 64 * h, 64), :],
            step - 1,
            *at_y(to),
        )

    dy_ring = RingGather(
        Links(dy_ss, dy_rs), y, at_y, lambda i: d_buf.at[pl.ds(x * 64 + i * 16, 16), :], lanes_half(512)
    )
    own_delta = dy_ring.block(y)
    for j in range(2):
        for k in range(2):
            own_delta[:, (2 * j + k) * BLK : (2 * j + k + 1) * BLK] = delta[:, j, k, :].astype(BF16)
    dy_ring.begin(own_delta)

    def gate_rows(other):
        at = pl.ds(pl.multiple_of(other * CAP, CAP), CAP)
        v = gate_pre[at, :].astype(F32)
        hg = hidden_grad[at, :].astype(F32)
        s = 1.0 / (1.0 + jnp.exp(-v))
        slope[at, :] = hg * (s * (1.0 + v * (1.0 - s)))
        u_send[at, :] = (hg * (v * s)).astype(BF16)

    def a2a_copy(src, dst, number, other):
        return pltpu.make_async_remote_copy(
            src_ref=src.at[pl.ds(pl.multiple_of(other * CAP, CAP), CAP), :],
            dst_ref=dst.at[pl.ds(pl.multiple_of(t * CAP, CAP), CAP), :],
            send_sem=a_ss.at[number],
            recv_sem=a_rs.at[number],
            device_id={"tok": other, "col": c},
            device_id_type=MESH,
        )

    def gate_step(i, carry):
        other = (t + i) % NT
        gate_rows(other)
        a2a_copy(u_send, u_buf, 0, other).start()
        return carry

    lax.fori_loop(1, NT, gate_step, 0)
    gate_rows(t)
    own_cap = pl.ds(pl.multiple_of(t * CAP, CAP), CAP)
    u_buf[own_cap, :] = u_send[own_cap, :]

    lane = lax.broadcasted_iota(jnp.int32, (ROWS, ROWS), 1)
    row = lax.broadcasted_iota(jnp.int32, (ROWS, ROWS), 0)
    goes = route[...]
    onehot = jnp.where(goes == lane, 1.0, 0.0)
    lower = jnp.where(lane < row, 1.0, 0.0)
    earlier = dot_nn(lower.astype(BF16), onehot.astype(BF16))
    slot = jnp.sum(earlier * onehot, axis=1, keepdims=True)
    target = goes.astype(F32) * CAP + slot
    eye = jnp.where(lane == row, 1.0, 0.0).astype(BF16)
    target_row = dot_tn(jnp.broadcast_to(target, (ROWS, ROWS)).astype(BF16), eye)
    wide = lax.broadcasted_iota(jnp.int32, (ROWS, NT * CAP), 1).astype(F32)
    pick = jnp.where(wide == target, 1.0, 0.0).astype(BF16)
    row_id = lax.broadcasted_iota(jnp.int32, (ROWS, 1), 0)
    live = jnp.where(row_id < RESP, lengths[0], lengths[1])
    row_weight = jnp.where(row_id % RESP < live, RESP / live.astype(F32), 0.0)

    dy_ring.forward()
    codes_ring.forward()
    dy_ring.finish()
    dx_ring = RingGather(
        Links(dx_ss, dx_rs), x, at_x, lambda i: d_buf.at[pl.ds(i * 64, 64), :], rows_half(32)
    )
    dx_ring.begin(dx_ring.block(x))

    pltpu.make_async_copy(
        u_buf.at[pl.ds(0, 15 * CAP), :], u_buf.at[pl.ds(0, 15 * CAP), :], a_rs.at[0]
    ).wait()
    up_grad = (row_weight * dot_nn(pick, u_buf[...])).astype(BF16)
    g_ring = RingGather(Links(g_ss, g_rs), y, at_y, lambda i: g_buf.at[i], g_half)
    own_g = g_buf.at[y]
    own_g[0:ROWS, :] = up_grad
    own_g[ROWS:GB, :] = jnp.concatenate([target_row[0 : GB - ROWS, :]] * 4, axis=1).astype(BF16)
    g_ring.begin(own_g)

    def choose_rows(i, carry):
        at = pl.ds(pl.multiple_of(i * 32, 32), 32)
        picked = [jnp.zeros((32, BLK), BF16)] * 4
        for block in range(D // BLK):
            held = rollout[at, block * BLK : (block + 1) * BLK]
            for q in range(4):
                on = jnp.full((32, BLK), is_same(brows[q // 2, q % 2], block), F32).astype(BF16)
                picked[q] = picked[q] + on * held
        for q in range(4):
            chosen_rows[q, at, :] = picked[q]
        return carry

    lax.fori_loop(0, 4, choose_rows, 0)
    for j in range(2):
        for k in range(2):
            chosen = chosen_rows[2 * j + k]
            grad = dot_tn(chosen, up_grad[:, j * BLK : (j + 1) * BLK]).astype(BF16)
            for yy in range(4):
                for xx in range(4):
                    q_part[
                        64 * xx + 16 * yy : 64 * xx + 16 * yy + 16,
                        (2 * j + k) * BLK : (2 * j + k + 1) * BLK,
                    ] = grad[64 * yy + 16 * xx : 64 * yy + 16 * xx + 16, :]
    q_ring = RingReduce(
        Links(q_ss, q_rs), x, at_x, lambda i: q_part.at[pl.ds(i * 64, 64), :], rows_half(32),
        q_first, q_stage, q_second,
    )
    q_ring.begin()

    for step in (1, 3, 2):
        source = (y + 4 - step) % 4
        mine = x_buf.at[pl.ds(source * ROWS + 64 * h, 64), :]
        x_links.wait(mine, step - 1)
        x_links.start(mine, mine, 3 + step - 1, t, 2 * z + 1 - h)
    x_buf[pl.ds(y * ROWS, ROWS), :] = rollout[:, pl.ds(pl.multiple_of(y * KS, KS), KS)]

    dx_ring.forward()
    g_ring.forward()
    codes_ring.finish()
    dx_ring.finish()

    def weight_rows(index, carry):
        block = y * 5 + index // 4
        part = index % 4
        for j in range(2):
            scale = scales[block, j]
            on = [is_same(brows[j, k], block) for k in range(2)]
            for xx in range(4):
                at = pl.ds(pl.multiple_of(index * 64 + xx * 16, 16), 16)
                held = pl.ds(pl.multiple_of(64 * xx + 16 * part, 16), 16)
                value = w_buf[at, j * BLK : (j + 1) * BLK].astype(F32) * scale
                for k in range(2):
                    q = 2 * j + k
                    value = value + on[k] * d_buf[held, q * BLK : (q + 1) * BLK].astype(F32)
                w_eff[at, j * BLK : (j + 1) * BLK] = value.astype(BF16)
        return carry

    lax.fori_loop(0, 20, weight_rows, 0)

    g_ring.finish()
    for yy in range(4):
        g_all[ROWS * yy : ROWS * (yy + 1), :] = g_buf[yy, 0:ROWS, :]

    s_links = Links(s_ss, s_rs)
    give_rows = pl.ds(pl.multiple_of(256 * (1 - h), 256), 256)
    keep_rows = pl.ds(pl.multiple_of(256 * h, 256), 256)
    for part in range(4):
        at = pl.ds(part * 320, 320)
        z_give[at, :] = dot_nt(w_eff[at, :], g_all[give_rows, :]).astype(BF16)
        s_links.start(z_give.at[at, :], z_take.at[at, :], part, t, 2 * z + 1 - h)

    def keep_part(part, carry):
        at = pl.ds(pl.multiple_of(part * 320, 320), 320)
        z_own[at, :] = dot_nt(w_eff[at, :], g_all[keep_rows, :])
        return carry

    lax.fori_loop(0, 4, keep_part, 0)

    for step in (1, 3, 2):
        source = (y + 4 - step) % 4
        x_links.wait(x_buf.at[pl.ds(source * ROWS + 64 * (1 - h), 64), :], 3 + step - 1)

    def up_rows(i, carry):
        at = pl.ds(pl.multiple_of(i * ROWS, ROWS), ROWS)
        h_part[at, :] = dot_nn(x_buf[at, :], w_eff[...]).astype(BF16)
        return carry

    lax.fori_loop(0, 4, up_rows, 0)
    h_ring = RingReduce(
        Links(h_ss, h_rs), y, at_y, lambda i: h_part.at[pl.ds(i * ROWS, ROWS), :], rows_half(64),
        h_first, h_stage, h_second,
    )
    h_ring.begin()

    for part in range(4):
        s_links.wait(z_take.at[pl.ds(part * 320, 320), :], part)
    up_z, down_z = (z + 1) % NZ, (z + NZ - 1) % NZ

    def own_chunk(d, half):
        at = pl.ds(pl.multiple_of(d * DCH, DCH), DCH)
        lanes = slice(half * 128, half * 128 + 128)
        return z_own[at, lanes] + z_take[at, lanes].astype(F32)

    def ring_copy(way, half, step):
        return pltpu.make_async_remote_copy(
            src_ref=z_send.at[way, half, step],
            dst_ref=z_recv.at[way, half, step],
            send_sem=z_ss.at[(way * 2 + half) * 8 + step],
            recv_sem=z_rs.at[(way * 2 + half) * 8 + step],
            device_id={"tok": t, "col": 2 * (up_z if way == 0 else down_z) + h},
            device_id_type=MESH,
        )

    steps_of = (8, 7)

    def ring_step(step):
        for half in range(2):
            for way in range(2):
                if step >= steps_of[way]:
                    continue
                d = (z + 8 - step) % NZ if way == 0 else (z + NZ - 7 + step) % NZ
                value = own_chunk(d, half)
                if step > 0:
                    ring_copy(way, half, step - 1).wait_recv()
                    value = value + z_recv[way, half, step - 1].astype(F32)
                z_send[way, half, step] = value.astype(BF16)
                ring_copy(way, half, step).start()

    ring_step(0)
    q_ring.forward()
    ring_step(1)
    h_ring.forward()
    ring_step(2)
    q_ring.finish()
    r_part[...] = q_ring.total(q_part[pl.ds(x * 64, 64), :].astype(F32)).astype(BF16)
    r_ring = RingReduce(
        Links(r_ss, r_rs), y, at_y, lambda i: r_part.at[pl.ds(i * 16, 16), :], lanes_half(512),
        r_first, r_stage, r_second,
    )
    r_ring.begin()
    ring_step(3)
    h_ring.finish()
    up_value = h_ring.total(h_part[pl.ds(y * ROWS, ROWS), :].astype(F32)) * row_weight
    slot_row = lax.broadcasted_iota(jnp.int32, (NT * CAP, ROWS), 0).astype(F32)
    put_slots = jnp.where(slot_row == target_row[0:1, :], 1.0, 0.0).astype(BF16)
    hs_send[...] = dot_nn(put_slots, up_value.astype(BF16)).astype(BF16)

    def h_step(i, carry):
        a2a_copy(hs_send, hs_buf, 1, (t + i) % NT).start()
        return carry

    lax.fori_loop(1, NT, h_step, 0)
    hs_buf[own_cap, :] = hs_send[own_cap, :]
    ring_step(4)
    r_ring.forward()
    ring_step(5)
    r_ring.finish()
    gradient = r_ring.total(r_part[pl.ds(pl.multiple_of(y * 16, 16), 16), :].astype(F32))

    tops = []
    for j in range(2):
        for k in range(2):
            q = 2 * j + k
            g = gradient[:, q * BLK : (q + 1) * BLK]
            new_m = beta_first * adam_m[:, j, k, :] + (1.0 - beta_first) * g
            new_v = beta_second * adam_v[:, j, k, :] + (1.0 - beta_second) * g * g
            corrected_m = new_m / (1.0 - beta_first**STEP)
            corrected_v = new_v / (1.0 - beta_second**STEP)
            new_delta = delta[:, j, k, :] - step_rate * corrected_m / (
                jnp.sqrt(corrected_v) + adam_eps
            )
            nm_out[:, j, k, :] = new_m
            nv_out[:, j, k, :] = new_v
            nd_out[:, j, k, :] = new_delta
            tops.append(jnp.max(jnp.abs(new_delta)))
    tile_row = lax.broadcasted_iota(jnp.int32, (8, 128), 0)
    tile = jnp.zeros((8, 128), F32)
    for q in range(4):
        tile = jnp.where(tile_row == q, tops[q], tile)
    m_send[...] = tile
    m_buf[t] = tile

    def m_copy(other):
        return pltpu.make_async_remote_copy(
            src_ref=m_send,
            dst_ref=m_buf.at[t],
            send_sem=a_ss.at[2],
            recv_sem=a_rs.at[2],
            device_id={"tok": other, "col": c},
            device_id_type=MESH,
        )

    def m_step(i, carry):
        m_copy((t + i) % NT).start()
        return carry

    lax.fori_loop(1, NT, m_step, 0)
    ring_step(6)

    pltpu.make_async_copy(
        hs_buf.at[pl.ds(0, 15 * CAP), :], hs_buf.at[pl.ds(0, 15 * CAP), :], a_rs.at[1]
    ).wait()
    gg_out[...] = (slope[...] * hs_buf[...].astype(F32)).astype(BF16)
    ring_step(7)

    pltpu.make_async_copy(m_buf.at[pl.ds(0, 15)], m_buf.at[pl.ds(0, 15)], a_rs.at[2]).wait()
    top = jnp.max(m_buf[...], axis=0)
    for j in range(2):
        for k in range(2):
            q = 2 * j + k
            scale = jnp.max(top[q : q + 1, :])
            ds_out[j, k] = scale
            dc_out[:, j, k, :] = (nd_out[:, j, k, :] / (scale + scale_eps)).astype(BF16)

    g_rows = []
    halves = []
    for half in range(2):
        ring_copy(0, half, 7).wait_recv()
        ring_copy(1, half, 6).wait_recv()
        total = own_chunk(z, half) + (
            z_recv[0, half, 7].astype(F32) + z_recv[1, half, 6].astype(F32)
        )
        halves.append(total.astype(BF16))
        g_rows.append(g_buf[2 * h + half, ROWS : ROWS + 16, 0:128].astype(F32)[0:1, :])
    chunk = jnp.concatenate(halves, axis=1)
    chunk = jnp.concatenate([chunk, jnp.zeros((128 - DCH, 256), BF16)], axis=0)
    wanted = jnp.concatenate(g_rows, axis=1)
    spot = lax.broadcasted_iota(jnp.int32, (2 * NT * CAP, 256), 0)
    side = lax.broadcasted_iota(jnp.int32, (2 * NT * CAP, 256), 1) // 128
    slot_of = ((spot // 32) * 16 + spot % 16).astype(F32)
    put_both = jnp.where((slot_of == wanted) & (side == (spot // 16) % 2), 1.0, 0.0).astype(BF16)
    f_send[...] = dot_nt(put_both, chunk).astype(BF16)
    to_col = 8 * y + z // 2

    def f_copy(other):
        return pltpu.make_async_remote_copy(
            src_ref=f_send.at[pl.ds(pl.multiple_of(other * 32, 32), 32), :],
            dst_ref=f_buf.at[z % 2, x * 2 + h],
            send_sem=a_ss.at[3],
            recv_sem=a_rs.at[3],
            device_id={"tok": other, "col": to_col},
            device_id_type=MESH,
        )

    stays = to_col == c

    @pl.when(stays)
    def _():
        f_buf[z % 2, x * 2 + h] = f_send[pl.ds(pl.multiple_of(t * 32, 32), 32), :]

    @pl.when(jnp.logical_not(stays))
    def _():
        f_copy(t).start()

    def f_step(i, carry):
        f_copy((t + i) % NT).start()
        return carry

    lax.fori_loop(1, NT, f_step, 0)

    from_row = c // 8
    mine_too = (from_row == y) & ((c % 8) == z // 2)

    @pl.when(mine_too)
    def _():
        pltpu.make_async_copy(
            f_send.at[pl.ds(0, 480), :], f_send.at[pl.ds(0, 480), :], a_rs.at[3]
        ).wait()

    @pl.when(jnp.logical_not(mine_too))
    def _():
        pltpu.make_async_copy(f_send, f_send, a_rs.at[3]).wait()

    lane_in = lax.broadcasted_iota(jnp.int32, (128, 256), 0)
    lane_out = lax.broadcasted_iota(jnp.int32, (128, 256), 1)
    place = [
        jnp.where((lane_in < DCH) & (lane_out == lane_in + DCH * side_of), 1.0, 0.0).astype(BF16)
        for side_of in range(2)
    ]
    for xx in range(4):
        for hh in range(2):
            got = dot_nn(f_buf[0, xx * 2 + hh], place[0]) + dot_nn(f_buf[1, xx * 2 + hh], place[1])
            got = got[:, 0:160].astype(BF16)
            for part in range(2):
                sender = 4 * (2 * hh + part) + xx
                ig_out[16 * sender : 16 * sender + 16, :] = got[16 * part : 16 * part + 16, :]

    for links in (
        codes_ring.links, x_links, dy_ring.links, dx_ring.links, g_ring.links,
        q_ring.links, r_ring.links, h_ring.links, s_links,
    ):
        links.drain()
    for way in range(2):
        for half in range(2):
            for step in range(steps_of[way]):
                ring_copy(way, half, step).wait_send()
    for number in range(2):
        pltpu.make_async_copy(
            u_buf.at[pl.ds(0, 15 * CAP), :], u_buf.at[pl.ds(0, 15 * CAP), :], a_ss.at[number]
        ).wait()
    pltpu.make_async_copy(m_buf.at[pl.ds(0, 15)], m_buf.at[pl.ds(0, 15)], a_ss.at[2]).wait()

    @pl.when(stays)
    def _():
        pltpu.make_async_copy(
            f_send.at[pl.ds(0, 480), :], f_send.at[pl.ds(0, 480), :], a_ss.at[3]
        ).wait()

    @pl.when(jnp.logical_not(stays))
    def _():
        pltpu.make_async_copy(f_send, f_send, a_ss.at[3]).wait()


def per_device(
    rollout, lengths, route, up_codes, up_scales, block_rows, delta, adam_m, adam_v, gate_pre, hidden_grad
):
    vmem = pl.BlockSpec(memory_space=pltpu.VMEM)
    smem = pl.BlockSpec(memory_space=pltpu.SMEM)
    dma = pltpu.SemaphoreType.DMA

    def bf(*shape):
        return pltpu.VMEM(shape, BF16)

    def fl(*shape):
        return pltpu.VMEM(shape, F32)

    scratch = [
        bf(256, COLS), bf(256, COLS), fl(256, COLS), bf(KS, COLS), bf(KS, COLS), bf(4 * ROWS, KS),
        bf(256, 1024), bf(4, GB, COLS), bf(4 * ROWS, COLS),
        bf(4 * ROWS, COLS), bf(2, 64, COLS), bf(2, 64, COLS), bf(2, ROWS, COLS),
        bf(256, COLS), bf(256, COLS),
        bf(256, 1024), bf(2, 32, 1024), bf(2, 32, 1024), bf(2, 64, 1024),
        bf(64, 1024), bf(2, 16, 512), bf(2, 16, 512), bf(2, 16, 1024),
        fl(8, 128), fl(NT, 8, 128), fl(KS, 256), bf(KS, 256), bf(KS, 256),
        bf(2, 2, 8, DCH, 128), bf(2, 2, 8, DCH, 128), bf(512, 128), bf(2, 8, 32, 128), bf(4, ROWS, BLK),
        dma((6,)), dma((6,)), dma((6,)), dma((6,)), dma((6,)), dma((6,)), dma((6,)), dma((6,)),
        dma((6,)), dma((6,)), dma((6,)), dma((6,)), dma((6,)), dma((6,)), dma((6,)), dma((6,)),
        dma((4,)), dma((4,)), dma((32,)), dma((32,)), dma((4,)), dma((4,)),
    ]
    block = jax.ShapeDtypeStruct(delta.shape, F32)
    return pl.pallas_call(
        kernel,
        out_shape=(
            jax.ShapeDtypeStruct((256, 160), BF16),
            jax.ShapeDtypeStruct((256, COLS), BF16),
            block,
            block,
            block,
            jax.ShapeDtypeStruct((2, 2), F32),
            jax.ShapeDtypeStruct(delta.shape, BF16),
        ),
        in_specs=[smem] * 3 + [vmem] * 8,
        out_specs=(vmem, vmem, vmem, vmem, vmem, smem, vmem),
        scratch_shapes=scratch,
        compiler_params=pltpu.CompilerParams(has_side_effects=True, vmem_limit_bytes=48 * 1024 * 1024),
        cost_estimate=pl.CostEstimate(flops=3 * 10**9, bytes_accessed=4 * 10**6, transcendentals=0),
    )(
        lengths, up_scales, block_rows, rollout, route, up_codes, delta, adam_m, adam_v, gate_pre, hidden_grad
    )


def solution(mesh):
    placed = (
        P("tok", None),
        P("tok"),
        P("tok", None),
        P("tok", "col"),
        P(None, "col"),
        P("col", None),
        P("tok", "col", None, None),
        P("tok", "col", None, None),
        P("tok", "col", None, None),
        P("tok", "col"),
        P("tok", "col"),
    )
    return jax.shard_map(
        per_device,
        mesh=mesh,
        in_specs=placed,
        out_specs=(
            P("tok", "col"),
            P("tok", "col"),
            P("tok", "col", None, None),
            P("tok", "col", None, None),
            P("tok", "col", None, None),
            P("col", None),
            P("tok", "col", None, None),
        ),
        check_vma=False,
    )
```

```python
import functools

import jax
import jax.numpy as jnp
from jax import lax
from jax.experimental import pallas as pl
from jax.experimental.pallas import tpu as pltpu
from jax.sharding import PartitionSpec as P

BLK = 256
VLIM = 62
RESP = 64
STEP = 1000
D = 5120
NT = 16
NZ = 16
CAP = 16
ROWS = 128
COLS = 512
KS = D // 4
CROWS = 320
DCH = KS // NZ
GB = 144

beta_first = 0.9
beta_second = 0.999
step_rate = 0.01
adam_eps = 1e-08
scale_eps = 1e-06

MESH = pl.DeviceIdType.MESH
F32 = jnp.float32
BF16 = jnp.bfloat16


def dot_nn(a, b):
    return lax.dot_general(a, b, (((1,), (0,)), ((), ())), preferred_element_type=F32)


def dot_nt(a, b):
    return lax.dot_general(a, b, (((1,), (1,)), ((), ())), preferred_element_type=F32)


def dot_tn(a, b):
    return lax.dot_general(a, b, (((0,), (0,)), ((), ())), preferred_element_type=F32)


def is_same(a, b):
    return (1 - jnp.minimum(jnp.abs(a - b), 1)).astype(F32)


class Links:
    def __init__(self, send, recv):
        self.send, self.recv = send, recv
        self.sent = []

    def copy(self, src, dst, number, tok, col):
        return pltpu.make_async_remote_copy(
            src_ref=src,
            dst_ref=dst,
            send_sem=self.send.at[number],
            recv_sem=self.recv.at[number],
            device_id={"tok": tok, "col": col},
            device_id_type=MESH,
        )

    def start(self, src, dst, number, tok, col):
        made = self.copy(src, dst, number, tok, col)
        made.start()
        self.sent.append(made)

    def wait(self, dst, number):
        pltpu.make_async_copy(dst, dst, self.recv.at[number]).wait()

    def drain(self):
        for made in self.sent:
            made.wait_send()


class RingGather:
    def __init__(self, links, me, device, block, half):
        self.links, self.block, self.half, self.device = links, block, half, device
        self.me = me
        self.right, self.left, self.far = (me + 1) % 4, (me + 3) % 4, (me + 2) % 4

    def put(self, src, index, part, number, to):
        self.links.start(self.half(src, part), self.half(self.block(index), part), number, *self.device(to))

    def got(self, index, part, number):
        self.links.wait(self.half(self.block(index), part), number)

    def begin(self, src):
        self.put(src, self.me, 0, 0, self.right)
        self.put(src, self.me, 1, 1, self.left)
        self.put(src, self.me, 1, 2, self.right)
        self.put(src, self.me, 0, 3, self.left)

    def forward(self):
        self.got(self.left, 0, 0)
        self.put(self.block(self.left), self.left, 0, 4, self.right)
        self.got(self.right, 1, 1)
        self.put(self.block(self.right), self.right, 1, 5, self.left)

    def finish(self):
        self.got(self.left, 1, 2)
        self.got(self.right, 0, 3)
        self.got(self.far, 0, 4)
        self.got(self.far, 1, 5)


class RingReduce:
    def __init__(self, links, me, device, part, half, first, stage, second):
        self.links, self.part, self.half, self.device = links, part, half, device
        self.first, self.stage, self.second = first, stage, second
        self.me = me
        self.right, self.left, self.far = (me + 1) % 4, (me + 3) % 4, (me + 2) % 4

    def put(self, src, dst, number, to):
        self.links.start(src, dst, number, *self.device(to))

    def begin(self):
        self.put(self.half(self.part(self.far), 0), self.first.at[0], 0, self.right)
        self.put(self.half(self.part(self.far), 1), self.first.at[1], 1, self.left)
        self.put(self.half(self.part(self.right), 1), self.half(self.second.at[0], 1), 2, self.right)
        self.put(self.half(self.part(self.left), 0), self.half(self.second.at[1], 0), 3, self.left)

    def forward(self):
        self.links.wait(self.first.at[0], 0)
        self.stage[0] = (
            self.half(self.part(self.right), 0)[...].astype(F32) + self.first[0].astype(F32)
        ).astype(BF16)
        self.put(self.stage.at[0], self.half(self.second.at[0], 0), 4, self.right)
        self.links.wait(self.first.at[1], 1)
        self.stage[1] = (
            self.half(self.part(self.left), 1)[...].astype(F32) + self.first[1].astype(F32)
        ).astype(BF16)
        self.put(self.stage.at[1], self.half(self.second.at[1], 1), 5, self.left)

    def finish(self):
        self.links.wait(self.half(self.second.at[0], 1), 2)
        self.links.wait(self.half(self.second.at[1], 0), 3)
        self.links.wait(self.half(self.second.at[0], 0), 4)
        self.links.wait(self.half(self.second.at[1], 1), 5)

    def total(self, own):
        return own + (self.second[0].astype(F32) + self.second[1].astype(F32))


def rows_half(size):
    def half(ref, part):
        return ref.at[pl.ds(part * size, size), :]

    return half


def lanes_half(size):
    def half(ref, part):
        return ref.at[:, pl.ds(part * size, size)]

    return half


def g_half(ref, part):
    return ref.at[pl.ds(0, 64), :] if part == 0 else ref.at[pl.ds(64, GB - 64), :]


def kernel(
    lengths_h, scales_h, brows_h, rollout_h, route_h, codes_h, delta_h, m_h, v_h, gate_h, hidden_h,
    ig_out, gg_out, nd_out, nm_out, nv_out, ds_out, dc_out,
    lengths, scales, brows, rollout, route, delta, adam_m, adam_v, gate_pre, hidden_grad,
    u_send, u_buf, slope, w_buf, w_eff, x_buf, d_buf, g_buf, g_all,
    h_part, h_first, h_stage, h_second, hs_send, hs_buf,
    q_part, q_first, q_stage, q_second, r_part, r_first, r_stage, r_second,
    m_send, m_buf, z_own, z_give, z_take, z_send, z_recv, f_send, f_buf, e_send, e_buf, chosen_rows, put_both,
    in_s, c_ss, c_rs, dy_ss, dy_rs, dx_ss, dx_rs, g_ss, g_rs, x_ss, x_rs, h_ss, h_rs,
    q_ss, q_rs, r_ss, r_rs, s_ss, s_rs, z_ss, z_rs, a_ss, a_rs, e_ss, e_rs,
):
    t = lax.axis_index("tok")
    c = lax.axis_index("col")
    y, x = t // 4, t % 4
    z, h = c // 2, c % 2
    sibling = 2 * z + 1 - h

    def at_x(other):
        return y * 4 + other, c

    def at_y(other):
        return other * 4 + x, c

    own_codes = w_buf.at[pl.ds(x * CROWS, CROWS), :]
    pairs = (
        (hidden_h, hidden_grad), (gate_h, gate_pre), (delta_h, delta), (codes_h, own_codes),
        (route_h, route), (lengths_h, lengths), (rollout_h, rollout), (brows_h, brows),
        (scales_h, scales), (m_h, adam_m), (v_h, adam_v),
    )
    loads = [pltpu.make_async_copy(src, dst, in_s.at[i]) for i, (src, dst) in enumerate(pairs)]
    for load in loads:
        load.start()

    def chunk_of(chip, row):
        return (chip + 22 - 4 * row) % NZ

    def end_of(row):
        chunk = chunk_of(z, row)
        return 2 * (4 * row + chunk // 4) + (chunk // 2) % 2

    def start_of(number):
        row = z // 4
        chunk = 4 * (z % 4) + 2 * h + number // 2
        return 2 * ((chunk + 10 + 4 * row) % NZ) + number % 2

    barrier = pltpu.get_barrier_semaphore()

    def greet(tok, col):
        pl.semaphore_signal(barrier, inc=1, device_id={"tok": tok, "col": col}, device_id_type=MESH)

    def greet_plane(i, carry):
        greet((t + i) % NT, c)
        return carry

    lax.fori_loop(1, NT, greet_plane, 0)
    greet(t, sibling)
    for distance in (1, 2, NZ - 2, NZ - 1):
        greet(t, 2 * ((z + distance) % NZ) + h)
    for number in range(4):
        for other in (end_of(number), start_of(number)):

            @pl.when(other != c)
            def _():
                greet(t, other)

    stays = end_of(z // 4) == c

    loads[0].wait()
    loads[1].wait()

    def gate_rows(i, carry):
        at = pl.ds(pl.multiple_of(i * 32, 32), 32)
        v = gate_pre[at, :].astype(F32)
        hg = hidden_grad[at, :].astype(F32)
        s = 1.0 / (1.0 + jnp.exp(-v))
        slope[at, :] = hg * (s * (1.0 + v * (1.0 - s)))
        u_send[at, :] = (hg * (v * s)).astype(BF16)
        return carry

    lax.fori_loop(0, 8, gate_rows, 0)

    dy_ring = RingGather(
        Links(dy_ss, dy_rs), y, at_y, lambda i: d_buf.at[pl.ds(x * 64 + i * 16, 16), :], lanes_half(512)
    )
    own_delta = dy_ring.block(y)
    loads[2].wait()
    for j in range(2):
        for k in range(2):
            own_delta[:, (2 * j + k) * BLK : (2 * j + k + 1) * BLK] = delta[:, j, k, :].astype(BF16)
    loads[3].wait()

    pl.semaphore_wait(barrier, jnp.where(stays, 26, 28))

    def a2a_copy(src, dst, number, other):
        return pltpu.make_async_remote_copy(
            src_ref=src.at[pl.ds(pl.multiple_of(other * CAP, CAP), CAP), :],
            dst_ref=dst.at[pl.ds(pl.multiple_of(t * CAP, CAP), CAP), :],
            send_sem=a_ss.at[number],
            recv_sem=a_rs.at[number],
            device_id={"tok": other, "col": c},
            device_id_type=MESH,
        )

    def u_step(i, carry):
        a2a_copy(u_send, u_buf, 0, (t + i) % NT).start()
        return carry

    lax.fori_loop(1, NT, u_step, 0)
    own_cap = pl.ds(pl.multiple_of(t * CAP, CAP), CAP)
    u_buf[own_cap, :] = u_send[own_cap, :]
    dy_ring.begin(own_delta)

    codes_ring = RingGather(
        Links(c_ss, c_rs), x, at_x, lambda i: w_buf.at[pl.ds(i * CROWS, CROWS), :], rows_half(CROWS // 2)
    )
    codes_ring.begin(own_codes)

    for load in loads[4:]:
        load.wait()
    lane = lax.broadcasted_iota(jnp.int32, (ROWS, ROWS), 1)
    row = lax.broadcasted_iota(jnp.int32, (ROWS, ROWS), 0)
    eye = jnp.where(lane == row, 1.0, 0.0).astype(BF16)
    route_rows = jnp.broadcast_to(route[...].astype(F32), (ROWS, ROWS)).astype(BF16)
    goes = dot_nt(eye, route_rows)
    onehot = jnp.where(goes == lane.astype(F32), 1.0, 0.0)
    lower = jnp.where(lane < row, 1.0, 0.0)
    earlier = dot_nn(lower.astype(BF16), onehot.astype(BF16))
    slot = jnp.sum(earlier * onehot, axis=1, keepdims=True)
    target = goes * CAP + slot
    target_row = dot_tn(target.astype(BF16), eye)
    wide = lax.broadcasted_iota(jnp.int32, (ROWS, NT * CAP), 1).astype(F32)
    pick = jnp.where(wide == target[:, 0:1], 1.0, 0.0).astype(BF16)
    slot_row = lax.broadcasted_iota(jnp.int32, (NT * CAP, ROWS), 0).astype(F32)
    put_slots = jnp.where(slot_row == target_row[0:1, :], 1.0, 0.0).astype(BF16)
    row_id = lax.broadcasted_iota(jnp.int32, (ROWS, 1), 0)
    live = jnp.where(row_id < RESP, lengths[0], lengths[1])
    row_weight = jnp.where(row_id % RESP < live, RESP / live.astype(F32), 0.0)

    pltpu.make_async_copy(
        u_buf.at[pl.ds(0, 15 * CAP), :], u_buf.at[pl.ds(0, 15 * CAP), :], a_rs.at[0]
    ).wait()
    up_grad = (row_weight * dot_nn(pick, u_buf[...])).astype(BF16)
    g_ring = RingGather(Links(g_ss, g_rs), y, at_y, lambda i: g_buf.at[i], g_half)
    own_g = g_buf.at[y]
    own_g[0:ROWS, :] = up_grad
    own_g[ROWS:GB, :] = jnp.concatenate([target_row[0 : GB - ROWS, :]] * 4, axis=1).astype(BF16)
    g_ring.begin(own_g)

    dy_ring.forward()
    codes_ring.forward()
    dy_ring.finish()
    dx_ring = RingGather(
        Links(dx_ss, dx_rs), x, at_x, lambda i: d_buf.at[pl.ds(i * 64, 64), :], rows_half(32)
    )
    dx_ring.begin(dx_ring.block(x))
    g_ring.forward()

    x_links = Links(x_ss, x_rs)
    for step in (1, 3, 2):
        to = (y + step) % 4
        x_links.start(
            rollout.at[pl.ds(64 * h, 64), pl.ds(pl.multiple_of(to * KS, KS), KS)],
            x_buf.at[pl.ds(y * ROWS + 64 * h, 64), :],
            step - 1,
            *at_y(to),
        )

    def choose_rows(i, carry):
        at = pl.ds(pl.multiple_of(i * 32, 32), 32)
        picked = [jnp.zeros((32, BLK), BF16)] * 4
        for block in range(D // BLK):
            held = rollout[at, block * BLK : (block + 1) * BLK]
            for q in range(4):
                on = jnp.full((32, BLK), is_same(brows[q // 2, q % 2], block), F32).astype(BF16)
                picked[q] = picked[q] + on * held
        for q in range(4):
            chosen_rows[q, at, :] = picked[q]
        return carry

    lax.fori_loop(0, 4, choose_rows, 0)
    for j in range(2):
        for k in range(2):
            chosen = chosen_rows[2 * j + k]
            grad = dot_tn(chosen, up_grad[:, j * BLK : (j + 1) * BLK]).astype(BF16)
            for yy in range(4):
                for xx in range(4):
                    q_part[
                        64 * xx + 16 * yy : 64 * xx + 16 * yy + 16,
                        (2 * j + k) * BLK : (2 * j + k + 1) * BLK,
                    ] = grad[64 * yy + 16 * xx : 64 * yy + 16 * xx + 16, :]
    q_ring = RingReduce(
        Links(q_ss, q_rs), x, at_x, lambda i: q_part.at[pl.ds(i * 64, 64), :], rows_half(32),
        q_first, q_stage, q_second,
    )
    q_ring.begin()
    x_buf[pl.ds(y * ROWS, ROWS), :] = rollout[:, pl.ds(pl.multiple_of(y * KS, KS), KS)]

    dx_ring.forward()
    dx_ring.finish()
    g_ring.finish()
    for yy in range(4):
        g_all[ROWS * yy : ROWS * (yy + 1), :] = g_buf[yy, 0:ROWS, :]

    def weight_rows(index, carry):
        block = y * 5 + index // 4
        part = index % 4
        for j in range(2):
            scale = scales[j, block]
            on = [is_same(brows[j, k], block) for k in range(2)]
            for xx in range(4):
                at = pl.ds(pl.multiple_of(index * 64 + xx * 16, 16), 16)
                held = pl.ds(pl.multiple_of(64 * xx + 16 * part, 16), 16)
                value = w_buf[at, j * BLK : (j + 1) * BLK].astype(F32) * scale
                for k in range(2):
                    q = 2 * j + k
                    value = value + on[k] * d_buf[held, q * BLK : (q + 1) * BLK].astype(F32)
                w_eff[at, j * BLK : (j + 1) * BLK] = value.astype(BF16)
        return carry

    s_links = Links(s_ss, s_rs)
    give_rows = pl.ds(pl.multiple_of(256 * (1 - h), 256), 256)
    keep_rows = pl.ds(pl.multiple_of(256 * h, 256), 256)
    for order, part in enumerate((x, codes_ring.left, codes_ring.right, codes_ring.far)):
        if order == 1:
            codes_ring.got(part, 1, 2)
        if order == 2:
            codes_ring.got(part, 0, 3)
        if order == 3:
            codes_ring.got(part, 0, 4)
            codes_ring.got(part, 1, 5)
        lax.fori_loop(5 * part, 5 * part + 5, weight_rows, 0)
        at = pl.ds(pl.multiple_of(part * CROWS, CROWS), CROWS)
        z_give[at, :] = dot_nt(w_eff[at, :], g_all[give_rows, :]).astype(BF16)
        s_links.start(z_give.at[at, :], z_take.at[at, :], order, t, sibling)
        z_own[at, :] = dot_nt(w_eff[at, :], g_all[keep_rows, :])

    wanted = jnp.concatenate(
        [g_buf[2 * h + half, ROWS : ROWS + 16, 0:128].astype(F32)[0:1, :] for half in range(2)], axis=1
    )
    spot = lax.broadcasted_iota(jnp.int32, (2 * NT * CAP, 256), 0)
    side = lax.broadcasted_iota(jnp.int32, (2 * NT * CAP, 256), 1) // 128
    slot_of = ((spot // 32) * 16 + spot % 16).astype(F32)
    put_both[...] = jnp.where((slot_of == wanted) & (side == (spot // 16) % 2), 1.0, 0.0).astype(BF16)

    for order, part in enumerate((x, codes_ring.left, codes_ring.right, codes_ring.far)):
        s_links.wait(z_take.at[pl.ds(pl.multiple_of(part * CROWS, CROWS), CROWS), :], order)

    def own_chunk(chip):
        at = pl.ds(pl.multiple_of(chunk_of(chip, y) * DCH, DCH), DCH)
        return z_own[at, :] + z_take[at, :].astype(F32)

    streams = (
        (8, NZ - 2, (2, 2, 2, 2)),
        (7, NZ - 2, (2, 2, 2, 1)),
        (NZ - 7, 2, (NZ - 2, NZ - 2, NZ - 2, NZ - 1)),
        (NZ - 6, 2, (NZ - 2, NZ - 2, NZ - 2)),
    )

    def ring_copy(number, step):
        return pltpu.make_async_remote_copy(
            src_ref=z_send.at[number, step],
            dst_ref=z_recv.at[number, step],
            send_sem=z_ss.at[number * 4 + step],
            recv_sem=z_rs.at[number * 4 + step],
            device_id={"tok": t, "col": 2 * ((z + streams[number][2][step]) % NZ) + h},
            device_id_type=MESH,
        )

    def ring_step(step):
        for number, (first, change, hops) in enumerate(streams):
            if step < len(hops):
                value = own_chunk((z + first + step * change) % NZ)
                if step > 0:
                    ring_copy(number, step - 1).wait_recv()
                    value = value + z_recv[number, step - 1].astype(F32)
                z_send[number, step] = value.astype(BF16)
                ring_copy(number, step).start()

    ring_step(0)

    for step in (1, 3, 2):
        source = (y + 4 - step) % 4
        mine = x_buf.at[pl.ds(source * ROWS + 64 * h, 64), :]
        x_links.wait(mine, step - 1)
        x_links.start(mine, mine, 3 + step - 1, t, sibling)
    q_ring.forward()
    ring_step(1)

    for step in (1, 3, 2):
        source = (y + 4 - step) % 4
        x_links.wait(x_buf.at[pl.ds(source * ROWS + 64 * (1 - h), 64), :], 3 + step - 1)

    def up_rows(i, carry):
        at = pl.ds(pl.multiple_of(i * ROWS, ROWS), ROWS)
        h_part[at, :] = dot_nn(x_buf[at, :], w_eff[...]).astype(BF16)
        return carry

    lax.fori_loop(0, 4, up_rows, 0)
    h_ring = RingReduce(
        Links(h_ss, h_rs), y, at_y, lambda i: h_part.at[pl.ds(i * ROWS, ROWS), :], rows_half(64),
        h_first, h_stage, h_second,
    )
    h_ring.begin()
    q_ring.finish()
    r_part[...] = q_ring.total(q_part[pl.ds(x * 64, 64), :].astype(F32)).astype(BF16)
    r_ring = RingReduce(
        Links(r_ss, r_rs), y, at_y, lambda i: r_part.at[pl.ds(i * 16, 16), :], lanes_half(512),
        r_first, r_stage, r_second,
    )
    r_ring.begin()
    ring_step(2)
    h_ring.forward()
    r_ring.forward()
    ring_step(3)
    h_ring.finish()
    up_value = h_ring.total(h_part[pl.ds(y * ROWS, ROWS), :].astype(F32)) * row_weight
    hs_send[...] = dot_nn(put_slots, up_value.astype(BF16)).astype(BF16)

    def h_step(i, carry):
        a2a_copy(hs_send, hs_buf, 1, (t + i) % NT).start()
        return carry

    lax.fori_loop(1, NT, h_step, 0)
    hs_buf[own_cap, :] = hs_send[own_cap, :]
    r_ring.finish()
    gradient = r_ring.total(r_part[pl.ds(pl.multiple_of(y * 16, 16), 16), :].astype(F32))

    tops = []
    for j in range(2):
        for k in range(2):
            q = 2 * j + k
            g = gradient[:, q * BLK : (q + 1) * BLK]
            new_m = beta_first * adam_m[:, j, k, :] + (1.0 - beta_first) * g
            new_v = beta_second * adam_v[:, j, k, :] + (1.0 - beta_second) * g * g
            corrected_m = new_m / (1.0 - beta_first**STEP)
            corrected_v = new_v / (1.0 - beta_second**STEP)
            new_delta = delta[:, j, k, :] - step_rate * corrected_m / (
                jnp.sqrt(corrected_v) + adam_eps
            )
            nm_out[:, j, k, :] = new_m
            nv_out[:, j, k, :] = new_v
            nd_out[:, j, k, :] = new_delta
            tops.append(jnp.max(jnp.abs(new_delta)))
    tile_row = lax.broadcasted_iota(jnp.int32, (8, 128), 0)
    tile = jnp.zeros((8, 128), F32)
    for q in range(4):
        tile = jnp.where(tile_row == q, tops[q], tile)
    m_send[...] = tile
    m_buf[t] = tile

    def m_copy(other):
        return pltpu.make_async_remote_copy(
            src_ref=m_send,
            dst_ref=m_buf.at[t],
            send_sem=a_ss.at[2],
            recv_sem=a_rs.at[2],
            device_id={"tok": other, "col": c},
            device_id_type=MESH,
        )

    def m_step(i, carry):
        m_copy((t + i) % NT).start()
        return carry

    lax.fori_loop(1, NT, m_step, 0)

    total = own_chunk(z)
    for number, (first, change, hops) in enumerate(streams):
        ring_copy(number, len(hops) - 1).wait_recv()
        total = total + z_recv[number, len(hops) - 1].astype(F32)
    chunk = jnp.concatenate([total.astype(BF16), jnp.zeros((128 - DCH, 256), BF16)], axis=0)
    f_send[...] = dot_nt(put_both[...], chunk).astype(BF16)

    def f_copy(other):
        return pltpu.make_async_remote_copy(
            src_ref=f_send.at[pl.ds(pl.multiple_of(other * 32, 32), 32), :],
            dst_ref=f_buf.at[pl.ds(pl.multiple_of(t * 32, 32), 32), :],
            send_sem=a_ss.at[3],
            recv_sem=a_rs.at[3],
            device_id={"tok": other, "col": c},
            device_id_type=MESH,
        )

    def f_step(i, carry):
        f_copy((t + i) % NT).start()
        return carry

    lax.fori_loop(1, NT, f_step, 0)
    own_f = pl.ds(pl.multiple_of(t * 32, 32), 32)
    f_buf[own_f, :] = f_send[own_f, :]

    pltpu.make_async_copy(
        hs_buf.at[pl.ds(0, 15 * CAP), :], hs_buf.at[pl.ds(0, 15 * CAP), :], a_rs.at[1]
    ).wait()
    gg_out[...] = (slope[...] * hs_buf[...].astype(F32)).astype(BF16)

    pltpu.make_async_copy(
        f_buf.at[pl.ds(0, 480), :], f_buf.at[pl.ds(0, 480), :], a_rs.at[3]
    ).wait()

    def e_copy(number):
        chunk_here = chunk_of(z, number)
        return pltpu.make_async_remote_copy(
            src_ref=e_send.at[number],
            dst_ref=e_buf.at[pl.ds((chunk_here % 2) * DCH, DCH), pl.ds(pl.multiple_of(h * 128, 128), 128)],
            send_sem=e_ss.at[number],
            recv_sem=e_rs.at[(chunk_here % 2) * 2 + h],
            device_id={"tok": t, "col": end_of(number)},
            device_id_type=MESH,
        )

    some_rows = jnp.where(
        lax.broadcasted_iota(jnp.int32, (DCH, 128), 0) == lax.broadcasted_iota(jnp.int32, (DCH, 128), 1), 1.0, 0.0
    ).astype(BF16)
    for number in range(4):
        held = f_buf[128 * number : 128 * number + 128, :]
        ordered = jnp.concatenate(
            [held[32 * xx + 16 * part : 32 * xx + 16 * part + 16] for part in range(2) for xx in range(4)],
            axis=0,
        )
        e_send[number] = dot_nt(some_rows, ordered).astype(BF16)
        away = end_of(number) != c

        @pl.when(away)
        def _():
            e_copy(number).start()

        @pl.when(jnp.logical_not(away))
        def _():
            e_buf[
                pl.ds(pl.multiple_of((chunk_of(z, number) % 2) * DCH, DCH), DCH),
                pl.ds(pl.multiple_of(h * 128, 128), 128),
            ] = e_send[number]

    pltpu.make_async_copy(m_buf.at[pl.ds(0, 15)], m_buf.at[pl.ds(0, 15)], a_rs.at[2]).wait()
    top = jnp.max(m_buf[...], axis=0)
    for j in range(2):
        for k in range(2):
            q = 2 * j + k
            scale = jnp.max(top[q : q + 1, :])
            ds_out[j, k] = scale
            dc_out[:, j, k, :] = (nd_out[:, j, k, :] / (scale + scale_eps)).astype(BF16)

    for number in range(4):
        other = start_of(number)

        @pl.when(other != c)
        def _():
            block = e_buf.at[
                pl.ds((number // 2) * DCH, DCH), pl.ds((number % 2) * 128, 128)
            ]
            pltpu.make_async_copy(block, block, e_rs.at[number]).wait()

    ig_out[...] = e_buf[...]

    for links in (
        codes_ring.links, x_links, dy_ring.links, dx_ring.links, g_ring.links,
        q_ring.links, r_ring.links, h_ring.links, s_links,
    ):
        links.drain()
    for number, (first, change, hops) in enumerate(streams):
        for step in range(len(hops)):
            ring_copy(number, step).wait_send()
    for number in range(2):
        pltpu.make_async_copy(
            u_buf.at[pl.ds(0, 15 * CAP), :], u_buf.at[pl.ds(0, 15 * CAP), :], a_ss.at[number]
        ).wait()
    pltpu.make_async_copy(m_buf.at[pl.ds(0, 15)], m_buf.at[pl.ds(0, 15)], a_ss.at[2]).wait()
    pltpu.make_async_copy(
        f_buf.at[pl.ds(0, 480), :], f_buf.at[pl.ds(0, 480), :], a_ss.at[3]
    ).wait()
    for number in range(4):

        @pl.when(end_of(number) != c)
        def _():
            e_copy(number).wait_send()


def per_device(
    rollout, lengths, route, up_codes, up_scales, block_rows, delta, adam_m, adam_v, gate_pre, hidden_grad
):
    vmem = pl.BlockSpec(memory_space=pltpu.VMEM)
    smem = pl.BlockSpec(memory_space=pltpu.SMEM)
    dma = pltpu.SemaphoreType.DMA

    def bf(*shape):
        return pltpu.VMEM(shape, BF16)

    def fl(*shape):
        return pltpu.VMEM(shape, F32)

    smem_of = pltpu.SMEM
    block4 = delta.shape
    scratch = [
        smem_of((2,), jnp.int32), smem_of((2, 20), F32), smem_of((2, 2), jnp.int32),
        bf(ROWS, D), pltpu.VMEM((1, ROWS), jnp.int32), fl(*block4), fl(*block4), fl(*block4),
        bf(256, COLS), bf(256, COLS),
        bf(256, COLS), bf(256, COLS), fl(256, COLS), bf(KS, COLS), bf(KS, COLS), bf(4 * ROWS, KS),
        bf(256, 1024), bf(4, GB, COLS), bf(4 * ROWS, COLS),
        bf(4 * ROWS, COLS), bf(2, 64, COLS), bf(2, 64, COLS), bf(2, ROWS, COLS),
        bf(256, COLS), bf(256, COLS),
        bf(256, 1024), bf(2, 32, 1024), bf(2, 32, 1024), bf(2, 64, 1024),
        bf(64, 1024), bf(2, 16, 512), bf(2, 16, 512), bf(2, 16, 1024),
        fl(8, 128), fl(NT, 8, 128), fl(KS, 256), bf(KS, 256), bf(KS, 256),
        bf(4, 4, DCH, 256), bf(4, 4, DCH, 256), bf(512, 128), bf(512, 128), bf(4, DCH, 128), bf(160, 256),
        bf(4, ROWS, BLK), bf(512, 256),
        dma((11,)),
        dma((6,)), dma((6,)), dma((6,)), dma((6,)), dma((6,)), dma((6,)), dma((6,)), dma((6,)),
        dma((6,)), dma((6,)), dma((6,)), dma((6,)), dma((6,)), dma((6,)), dma((6,)), dma((6,)),
        dma((4,)), dma((4,)), dma((16,)), dma((16,)), dma((4,)), dma((4,)), dma((4,)), dma((4,)),
    ]
    block = jax.ShapeDtypeStruct(delta.shape, F32)
    outs = pl.pallas_call(
        kernel,
        out_shape=(
            jax.ShapeDtypeStruct((160, 256), BF16),
            jax.ShapeDtypeStruct((256, COLS), BF16),
            block,
            block,
            block,
            jax.ShapeDtypeStruct((2, 2), F32),
            jax.ShapeDtypeStruct(delta.shape, BF16),
        ),
        in_specs=[pl.BlockSpec(memory_space=pl.ANY)] * 11,
        out_specs=(vmem, vmem, vmem, vmem, vmem, smem, vmem),
        scratch_shapes=scratch,
        compiler_params=pltpu.CompilerParams(
            collective_id=0, has_side_effects=True, vmem_limit_bytes=VLIM * 1024 * 1024
        ),
        cost_estimate=pl.CostEstimate(flops=3 * 10**9, bytes_accessed=4 * 10**6, transcendentals=0),
    )(
        lengths, up_scales.T, block_rows, rollout, route.T, up_codes, delta, adam_m, adam_v, gate_pre, hidden_grad
    )
    return (outs[0].T,) + tuple(outs[1:])


def solution(mesh):
    placed = (
        P("tok", None),
        P("tok"),
        P("tok", None),
        P("tok", "col"),
        P(None, "col"),
        P("col", None),
        P("tok", "col", None, None),
        P("tok", "col", None, None),
        P("tok", "col", None, None),
        P("tok", "col"),
        P("tok", "col"),
    )
    return jax.shard_map(
        per_device,
        mesh=mesh,
        in_specs=placed,
        out_specs=(
            P("tok", "col"),
            P("tok", "col"),
            P("tok", "col", None, None),
            P("tok", "col", None, None),
            P("tok", "col", None, None),
            P("col", None),
            P("tok", "col", None, None),
        ),
        check_vma=False,
    )
```

```python
import functools

import jax
import jax.numpy as jnp
from jax import lax
from jax.experimental import pallas as pl
from jax.experimental.pallas import tpu as pltpu
from jax.sharding import PartitionSpec as P

BLK = 256
VLIM = 62
VLIM2 = 62
RESP = 64
STEP = 1000
D = 5120
NT = 16
NZ = 16
CAP = 16
ROWS = 128
COLS = 512
KS = D // 4
CROWS = 320
DCH = KS // NZ
GB = 144

beta_first = 0.9
beta_second = 0.999
step_rate = 0.01
adam_eps = 1e-08
scale_eps = 1e-06

MESH = pl.DeviceIdType.MESH
F32 = jnp.float32
BF16 = jnp.bfloat16


def dot_nn(a, b):
    return lax.dot_general(a, b, (((1,), (0,)), ((), ())), preferred_element_type=F32)


def dot_nt(a, b):
    return lax.dot_general(a, b, (((1,), (1,)), ((), ())), preferred_element_type=F32)


def dot_tn(a, b):
    return lax.dot_general(a, b, (((0,), (0,)), ((), ())), preferred_element_type=F32)


def is_same(a, b):
    return (1 - jnp.minimum(jnp.abs(a - b), 1)).astype(F32)


class Links:
    def __init__(self, send, recv):
        self.send, self.recv = send, recv
        self.sent = []

    def copy(self, src, dst, number, tok, col):
        return pltpu.make_async_remote_copy(
            src_ref=src,
            dst_ref=dst,
            send_sem=self.send.at[number],
            recv_sem=self.recv.at[number],
            device_id={"tok": tok, "col": col},
            device_id_type=MESH,
        )

    def start(self, src, dst, number, tok, col):
        made = self.copy(src, dst, number, tok, col)
        made.start()
        self.sent.append(made)

    def wait(self, dst, number):
        pltpu.make_async_copy(dst, dst, self.recv.at[number]).wait()

    def drain(self):
        for made in self.sent:
            made.wait_send()


class RingGather:
    def __init__(self, links, me, device, block, half):
        self.links, self.block, self.half, self.device = links, block, half, device
        self.me = me
        self.right, self.left, self.far = (me + 1) % 4, (me + 3) % 4, (me + 2) % 4

    def put(self, src, index, part, number, to):
        self.links.start(self.half(src, part), self.half(self.block(index), part), number, *self.device(to))

    def got(self, index, part, number):
        self.links.wait(self.half(self.block(index), part), number)

    def begin(self, src):
        self.put(src, self.me, 0, 0, self.right)
        self.put(src, self.me, 1, 1, self.left)
        self.put(src, self.me, 1, 2, self.right)
        self.put(src, self.me, 0, 3, self.left)

    def forward(self):
        self.got(self.left, 0, 0)
        self.put(self.block(self.left), self.left, 0, 4, self.right)
        self.got(self.right, 1, 1)
        self.put(self.block(self.right), self.right, 1, 5, self.left)

    def finish(self):
        self.got(self.left, 1, 2)
        self.got(self.right, 0, 3)
        self.got(self.far, 0, 4)
        self.got(self.far, 1, 5)


class DirectGather:
    def __init__(self, links, me, device, block):
        self.links, self.me, self.device, self.block = links, me, device, block

    def begin(self):
        for step in (1, 3, 2):
            own = self.block(self.me)
            self.links.start(own, own, step - 1, *self.device((self.me + step) % 4))

    def finish(self):
        for step in (1, 3, 2):
            self.links.wait(self.block((self.me + 4 - step) % 4), step - 1)


class RingReduce:
    def __init__(self, links, me, device, part, half, first, stage, second):
        self.links, self.part, self.half, self.device = links, part, half, device
        self.first, self.stage, self.second = first, stage, second
        self.me = me
        self.right, self.left, self.far = (me + 1) % 4, (me + 3) % 4, (me + 2) % 4

    def put(self, src, dst, number, to):
        self.links.start(src, dst, number, *self.device(to))

    def begin(self):
        self.put(self.half(self.part(self.far), 0), self.first.at[0], 0, self.right)
        self.put(self.half(self.part(self.far), 1), self.first.at[1], 1, self.left)
        self.put(self.half(self.part(self.right), 1), self.half(self.second.at[0], 1), 2, self.right)
        self.put(self.half(self.part(self.left), 0), self.half(self.second.at[1], 0), 3, self.left)

    def forward(self):
        self.links.wait(self.first.at[0], 0)
        self.stage[0] = (
            self.half(self.part(self.right), 0)[...].astype(F32) + self.first[0].astype(F32)
        ).astype(BF16)
        self.put(self.stage.at[0], self.half(self.second.at[0], 0), 4, self.right)
        self.links.wait(self.first.at[1], 1)
        self.stage[1] = (
            self.half(self.part(self.left), 1)[...].astype(F32) + self.first[1].astype(F32)
        ).astype(BF16)
        self.put(self.stage.at[1], self.half(self.second.at[1], 1), 5, self.left)

    def finish(self):
        self.links.wait(self.half(self.second.at[0], 1), 2)
        self.links.wait(self.half(self.second.at[1], 0), 3)
        self.links.wait(self.half(self.second.at[0], 0), 4)
        self.links.wait(self.half(self.second.at[1], 1), 5)

    def total(self, own):
        return own + (self.second[0].astype(F32) + self.second[1].astype(F32))


def rows_half(size):
    def half(ref, part):
        return ref.at[pl.ds(part * size, size), :]

    return half


def lanes_half(size):
    def half(ref, part):
        return ref.at[:, pl.ds(part * size, size)]

    return half


def g_half(ref, part):
    return ref.at[pl.ds(0, 64), :] if part == 0 else ref.at[pl.ds(64, GB - 64), :]


def kernel(
    lengths_h, scales_h, brows_h, rollout_h, route_h, codes_h, delta_h, m_h, v_h, gate_h, hidden_h,
    ig_out, gg_out, nd_out, nm_out, nv_out, ds_out, dc_out,
    lengths, scales, brows, rollout, route, delta, adam_m, adam_v, gate_pre, hidden_grad,
    u_send, u_buf, slope, w_buf, w_eff, x_buf, d_buf, g_buf, g_all,
    h_part, h_first, h_stage, h_second, hs_send, hs_buf,
    q_part, q_first, q_stage, q_second, r_part, r_first, r_stage, r_second,
    m_send, m_buf, z_own, z_give, z_take, z_send, z_recv, f_send, f_buf, e_send, e_buf, chosen_rows, put_both,
    in_s, c_ss, c_rs, dy_ss, dy_rs, dx_ss, dx_rs, g_ss, g_rs, x_ss, x_rs, h_ss, h_rs,
    q_ss, q_rs, r_ss, r_rs, s_ss, s_rs, z_ss, z_rs, a_ss, a_rs, e_ss, e_rs,
):
    t = lax.axis_index("tok")
    c = lax.axis_index("col")
    y, x = t // 4, t % 4
    z, h = c // 2, c % 2
    sibling = 2 * z + 1 - h

    def at_x(other):
        return y * 4 + other, c

    def at_y(other):
        return other * 4 + x, c

    own_codes = w_buf.at[pl.ds(x * CROWS, CROWS), :]
    pairs = (
        (hidden_h, hidden_grad), (gate_h, gate_pre), (delta_h, delta), (codes_h, own_codes),
        (route_h, route), (lengths_h, lengths), (rollout_h, rollout), (brows_h, brows),
        (scales_h, scales), (m_h, adam_m), (v_h, adam_v),
    )
    loads = [pltpu.make_async_copy(src, dst, in_s.at[i]) for i, (src, dst) in enumerate(pairs)]
    for load in loads:
        load.start()

    def chunk_of(chip, row):
        return (chip + 22 - 4 * row) % NZ

    def end_of(row):
        chunk = chunk_of(z, row)
        return 2 * (4 * row + chunk // 4) + (chunk // 2) % 2

    def start_of(number):
        row = z // 4
        chunk = 4 * (z % 4) + 2 * h + number // 2
        return 2 * ((chunk + 10 + 4 * row) % NZ) + number % 2

    barrier = pltpu.get_barrier_semaphore()

    def greet(tok, col):
        pl.semaphore_signal(barrier, inc=1, device_id={"tok": tok, "col": col}, device_id_type=MESH)

    def greet_plane(i, carry):
        greet((t + i) % NT, c)
        return carry

    lax.fori_loop(1, NT, greet_plane, 0)
    greet(t, sibling)
    for distance in (1, 2, NZ - 2, NZ - 1):
        greet(t, 2 * ((z + distance) % NZ) + h)
    for number in range(4):
        for other in (end_of(number), start_of(number)):

            @pl.when(other != c)
            def _():
                greet(t, other)

    stays = end_of(z // 4) == c

    loads[0].wait()
    loads[1].wait()

    def gate_rows(i, carry):
        at = pl.ds(pl.multiple_of(i * 32, 32), 32)
        v = gate_pre[at, :].astype(F32)
        hg = hidden_grad[at, :].astype(F32)
        s = 1.0 / (1.0 + jnp.exp(-v))
        slope[at, :] = hg * (s * (1.0 + v * (1.0 - s)))
        u_send[at, :] = (hg * (v * s)).astype(BF16)
        return carry

    lax.fori_loop(0, 8, gate_rows, 0)

    dx_ring = DirectGather(
        Links(dx_ss, dx_rs), x, at_x, lambda i: d_buf.at[pl.ds(y * 64 + i * 16, 16), :]
    )
    own_delta = dx_ring.block(x)
    loads[2].wait()
    for j in range(2):
        for k in range(2):
            own_delta[:, (2 * j + k) * BLK : (2 * j + k + 1) * BLK] = delta[:, j, k, :].astype(BF16)
    loads[3].wait()

    pl.semaphore_wait(barrier, jnp.where(stays, 26, 28))

    dx_ring.begin()

    def a2a_copy(src, dst, number, other):
        return pltpu.make_async_remote_copy(
            src_ref=src.at[pl.ds(pl.multiple_of(other * CAP, CAP), CAP), :],
            dst_ref=dst.at[pl.ds(pl.multiple_of(t * CAP, CAP), CAP), :],
            send_sem=a_ss.at[number],
            recv_sem=a_rs.at[number],
            device_id={"tok": other, "col": c},
            device_id_type=MESH,
        )

    def u_step(i, carry):
        a2a_copy(u_send, u_buf, 0, (t + i) % NT).start()
        return carry

    lax.fori_loop(1, NT, u_step, 0)
    own_cap = pl.ds(pl.multiple_of(t * CAP, CAP), CAP)
    u_buf[own_cap, :] = u_send[own_cap, :]

    codes_ring = RingGather(
        Links(c_ss, c_rs), x, at_x, lambda i: w_buf.at[pl.ds(i * CROWS, CROWS), :], rows_half(CROWS // 2)
    )
    codes_ring.begin(own_codes)

    for load in loads[4:]:
        load.wait()
    lane = lax.broadcasted_iota(jnp.int32, (ROWS, ROWS), 1)
    row = lax.broadcasted_iota(jnp.int32, (ROWS, ROWS), 0)
    eye = jnp.where(lane == row, 1.0, 0.0).astype(BF16)
    route_rows = jnp.broadcast_to(route[...].astype(F32), (ROWS, ROWS)).astype(BF16)
    goes = dot_nt(eye, route_rows)
    onehot = jnp.where(goes == lane.astype(F32), 1.0, 0.0)
    lower = jnp.where(lane < row, 1.0, 0.0)
    earlier = dot_nn(lower.astype(BF16), onehot.astype(BF16))
    slot = jnp.sum(earlier * onehot, axis=1, keepdims=True)
    target = goes * CAP + slot
    target_row = dot_tn(target.astype(BF16), eye)
    wide = lax.broadcasted_iota(jnp.int32, (ROWS, NT * CAP), 1).astype(F32)
    pick = jnp.where(wide == target[:, 0:1], 1.0, 0.0).astype(BF16)
    slot_row = lax.broadcasted_iota(jnp.int32, (NT * CAP, ROWS), 0).astype(F32)
    put_slots = jnp.where(slot_row == target_row[0:1, :], 1.0, 0.0).astype(BF16)
    row_id = lax.broadcasted_iota(jnp.int32, (ROWS, 1), 0)
    live = jnp.where(row_id < RESP, lengths[0], lengths[1])
    row_weight = jnp.where(row_id % RESP < live, RESP / live.astype(F32), 0.0)

    dx_ring.finish()
    dy_ring = RingGather(
        Links(dy_ss, dy_rs), y, at_y, lambda i: d_buf.at[pl.ds(i * 64, 64), :], rows_half(32)
    )
    dy_ring.begin(dy_ring.block(y))

    pltpu.make_async_copy(
        u_buf.at[pl.ds(0, 15 * CAP), :], u_buf.at[pl.ds(0, 15 * CAP), :], a_rs.at[0]
    ).wait()
    up_grad = (row_weight * dot_nn(pick, u_buf[...])).astype(BF16)
    g_ring = RingGather(Links(g_ss, g_rs), y, at_y, lambda i: g_buf.at[i], g_half)
    own_g = g_buf.at[y]
    own_g[0:ROWS, :] = up_grad
    own_g[ROWS:GB, :] = jnp.concatenate([target_row[0 : GB - ROWS, :]] * 4, axis=1).astype(BF16)
    g_ring.begin(own_g)

    codes_ring.forward()
    dy_ring.forward()
    g_ring.forward()

    x_links = Links(x_ss, x_rs)
    for step in (1, 3, 2):
        to = (y + step) % 4
        x_links.start(
            rollout.at[pl.ds(64 * h, 64), pl.ds(pl.multiple_of(to * KS, KS), KS)],
            x_buf.at[pl.ds(y * ROWS + 64 * h, 64), :],
            step - 1,
            *at_y(to),
        )

    def choose_rows(i, carry):
        at = pl.ds(pl.multiple_of(i * 32, 32), 32)
        picked = [jnp.zeros((32, BLK), BF16)] * 4
        for block in range(D // BLK):
            held = rollout[at, block * BLK : (block + 1) * BLK]
            for q in range(4):
                on = jnp.full((32, BLK), is_same(brows[q // 2, q % 2], block), F32).astype(BF16)
                picked[q] = picked[q] + on * held
        for q in range(4):
            chosen_rows[q, at, :] = picked[q]
        return carry

    lax.fori_loop(0, 4, choose_rows, 0)
    for j in range(2):
        for k in range(2):
            chosen = chosen_rows[2 * j + k]
            grad = dot_tn(chosen, up_grad[:, j * BLK : (j + 1) * BLK]).astype(BF16)
            for yy in range(4):
                for xx in range(4):
                    q_part[
                        64 * xx + 16 * yy : 64 * xx + 16 * yy + 16,
                        (2 * j + k) * BLK : (2 * j + k + 1) * BLK,
                    ] = grad[64 * yy + 16 * xx : 64 * yy + 16 * xx + 16, :]
    q_ring = RingReduce(
        Links(q_ss, q_rs), x, at_x, lambda i: q_part.at[pl.ds(i * 64, 64), :], rows_half(32),
        q_first, q_stage, q_second,
    )
    q_ring.begin()
    x_buf[pl.ds(y * ROWS, ROWS), :] = rollout[:, pl.ds(pl.multiple_of(y * KS, KS), KS)]

    dy_ring.finish()
    g_ring.finish()
    for yy in range(4):
        g_all[ROWS * yy : ROWS * (yy + 1), :] = g_buf[yy, 0:ROWS, :]

    def weight_rows(index, carry):
        block = y * 5 + index // 4
        part = index % 4
        for j in range(2):
            scale = scales[j, block]
            on = [is_same(brows[j, k], block) for k in range(2)]
            at = pl.ds(pl.multiple_of(index * 64, 64), 64)
            held = pl.ds(pl.multiple_of(64 * part, 64), 64)
            value = w_buf[at, j * BLK : (j + 1) * BLK].astype(F32) * scale
            for k in range(2):
                q = 2 * j + k
                value = value + on[k] * d_buf[held, q * BLK : (q + 1) * BLK].astype(F32)
            w_eff[at, j * BLK : (j + 1) * BLK] = value.astype(BF16)
        return carry

    s_links = Links(s_ss, s_rs)
    give_rows = pl.ds(pl.multiple_of(256 * (1 - h), 256), 256)
    keep_rows = pl.ds(pl.multiple_of(256 * h, 256), 256)
    for order, part in enumerate((x, codes_ring.left, codes_ring.right, codes_ring.far)):
        if order == 1:
            codes_ring.got(part, 1, 2)
        if order == 2:
            codes_ring.got(part, 0, 3)
        if order == 3:
            codes_ring.got(part, 0, 4)
            codes_ring.got(part, 1, 5)
        lax.fori_loop(5 * part, 5 * part + 5, weight_rows, 0)
        at = pl.ds(pl.multiple_of(part * CROWS, CROWS), CROWS)
        z_give[at, :] = dot_nt(w_eff[at, :], g_all[give_rows, :]).astype(BF16)
        s_links.start(z_give.at[at, :], z_take.at[at, :], order, t, sibling)
        z_own[at, :] = dot_nt(w_eff[at, :], g_all[keep_rows, :])

    wanted = jnp.concatenate(
        [g_buf[2 * h + half, ROWS : ROWS + 16, 0:128].astype(F32)[0:1, :] for half in range(2)], axis=1
    )
    spot = lax.broadcasted_iota(jnp.int32, (2 * NT * CAP, 256), 0)
    side = lax.broadcasted_iota(jnp.int32, (2 * NT * CAP, 256), 1) // 128
    slot_of = ((spot // 32) * 16 + spot % 16).astype(F32)
    put_both[...] = jnp.where((slot_of == wanted) & (side == (spot // 16) % 2), 1.0, 0.0).astype(BF16)

    for order, part in enumerate((x, codes_ring.left, codes_ring.right, codes_ring.far)):
        s_links.wait(z_take.at[pl.ds(pl.multiple_of(part * CROWS, CROWS), CROWS), :], order)

    def own_chunk(chip):
        at = pl.ds(pl.multiple_of(chunk_of(chip, y) * DCH, DCH), DCH)
        return z_own[at, :] + z_take[at, :].astype(F32)

    streams = ((2, 8, NZ - 2, 4), (NZ - 2, NZ - 6, 2, 3), (1, 7, NZ - 2, 4), (NZ - 1, NZ - 7, 2, 4))

    def ring_copy(number, step):
        return pltpu.make_async_remote_copy(
            src_ref=z_send.at[number, step],
            dst_ref=z_recv.at[number, step],
            send_sem=z_ss.at[number * 4 + step],
            recv_sem=z_rs.at[number * 4 + step],
            device_id={"tok": t, "col": 2 * ((z + streams[number][0]) % NZ) + h},
            device_id_type=MESH,
        )

    def ring_send(number, step, *joins):
        hops, first, change, steps = streams[number]
        value = own_chunk((z + first + step * change) % NZ)
        for stream, index in joins:
            ring_copy(stream, index).wait_recv()
            value = value + z_recv[stream, index].astype(F32)
        z_send[number, step] = value.astype(BF16)
        ring_copy(number, step).start()

    def ring_step(step):
        if step == 0:
            ring_send(0, 0)
            ring_send(3, 0)
            ring_send(2, 0)
            ring_send(3, 1)
            ring_send(2, 1)
            ring_send(1, 0, (3, 0))
        else:
            ring_send(0, step, (2, step - 1), (0, step - 1))
            if step < 3:
                ring_send(1, step, (3, step), (1, step - 1))
                ring_send(3, step + 1)
                ring_send(2, step + 1)

    ring_step(0)
    q_ring.forward()
    for step in (1, 3, 2):
        source = (y + 4 - step) % 4
        mine = x_buf.at[pl.ds(source * ROWS + 64 * h, 64), :]
        x_links.wait(mine, step - 1)
        x_links.start(mine, mine, 3 + step - 1, t, sibling)
    ring_step(1)
    q_ring.finish()
    r_part[...] = q_ring.total(q_part[pl.ds(x * 64, 64), :].astype(F32)).astype(BF16)
    r_ring = RingReduce(
        Links(r_ss, r_rs), y, at_y, lambda i: r_part.at[pl.ds(i * 16, 16), :], lanes_half(512),
        r_first, r_stage, r_second,
    )
    r_ring.begin()
    ring_step(2)

    for step in (1, 3, 2):
        source = (y + 4 - step) % 4
        x_links.wait(x_buf.at[pl.ds(source * ROWS + 64 * (1 - h), 64), :], 3 + step - 1)

    def up_rows(i, carry):
        at = pl.ds(pl.multiple_of(i * ROWS, ROWS), ROWS)
        h_part[at, :] = dot_nn(x_buf[at, :], w_eff[...]).astype(BF16)
        return carry

    lax.fori_loop(0, 4, up_rows, 0)
    h_ring = RingReduce(
        Links(h_ss, h_rs), y, at_y, lambda i: h_part.at[pl.ds(i * ROWS, ROWS), :], rows_half(64),
        h_first, h_stage, h_second,
    )
    h_ring.begin()
    r_ring.forward()
    ring_step(3)
    r_ring.finish()
    gradient = r_ring.total(r_part[pl.ds(pl.multiple_of(y * 16, 16), 16), :].astype(F32))

    tops = []
    for j in range(2):
        for k in range(2):
            q = 2 * j + k
            g = gradient[:, q * BLK : (q + 1) * BLK]
            new_m = beta_first * adam_m[:, j, k, :] + (1.0 - beta_first) * g
            new_v = beta_second * adam_v[:, j, k, :] + (1.0 - beta_second) * g * g
            corrected_m = new_m / (1.0 - beta_first**STEP)
            corrected_v = new_v / (1.0 - beta_second**STEP)
            new_delta = delta[:, j, k, :] - step_rate * corrected_m / (
                jnp.sqrt(corrected_v) + adam_eps
            )
            nm_out[:, j, k, :] = new_m
            nv_out[:, j, k, :] = new_v
            nd_out[:, j, k, :] = new_delta
            tops.append(jnp.max(jnp.abs(new_delta)))
    tile_row = lax.broadcasted_iota(jnp.int32, (8, 128), 0)
    tile = jnp.zeros((8, 128), F32)
    for q in range(4):
        tile = jnp.where(tile_row == q, tops[q], tile)
    m_send[...] = tile
    m_buf[t] = tile

    def m_copy(other):
        return pltpu.make_async_remote_copy(
            src_ref=m_send,
            dst_ref=m_buf.at[t],
            send_sem=a_ss.at[2],
            recv_sem=a_rs.at[2],
            device_id={"tok": other, "col": c},
            device_id_type=MESH,
        )

    def m_step(i, carry):
        m_copy((t + i) % NT).start()
        return carry

    lax.fori_loop(1, NT, m_step, 0)

    total = own_chunk(z)
    for number, (hops, first, change, steps) in enumerate(streams):
        ring_copy(number, steps - 1).wait_recv()
        total = total + z_recv[number, steps - 1].astype(F32)
    chunk = jnp.concatenate([total.astype(BF16), jnp.zeros((128 - DCH, 256), BF16)], axis=0)
    f_send[...] = dot_nt(put_both[...], chunk).astype(BF16)

    def f_copy(other):
        return pltpu.make_async_remote_copy(
            src_ref=f_send.at[pl.ds(pl.multiple_of(other * 32, 32), 32), :],
            dst_ref=f_buf.at[pl.ds(pl.multiple_of(t * 32, 32), 32), :],
            send_sem=a_ss.at[3],
            recv_sem=a_rs.at[3],
            device_id={"tok": other, "col": c},
            device_id_type=MESH,
        )

    def f_step(i, carry):
        f_copy((t + i) % NT).start()
        return carry

    lax.fori_loop(1, NT, f_step, 0)
    own_f = pl.ds(pl.multiple_of(t * 32, 32), 32)
    f_buf[own_f, :] = f_send[own_f, :]

    h_ring.forward()
    h_ring.finish()
    up_value = h_ring.total(h_part[pl.ds(y * ROWS, ROWS), :].astype(F32)) * row_weight
    hs_send[...] = dot_nn(put_slots, up_value.astype(BF16)).astype(BF16)

    def h_step(i, carry):
        a2a_copy(hs_send, hs_buf, 1, (t + i) % NT).start()
        return carry

    lax.fori_loop(1, NT, h_step, 0)
    hs_buf[own_cap, :] = hs_send[own_cap, :]

    pltpu.make_async_copy(
        f_buf.at[pl.ds(0, 480), :], f_buf.at[pl.ds(0, 480), :], a_rs.at[3]
    ).wait()

    def e_copy(number):
        chunk_here = chunk_of(z, number)
        return pltpu.make_async_remote_copy(
            src_ref=e_send.at[number],
            dst_ref=e_buf.at[pl.ds((chunk_here % 2) * DCH, DCH), pl.ds(pl.multiple_of(h * 128, 128), 128)],
            send_sem=e_ss.at[number],
            recv_sem=e_rs.at[(chunk_here % 2) * 2 + h],
            device_id={"tok": t, "col": end_of(number)},
            device_id_type=MESH,
        )

    some_rows = jnp.where(
        lax.broadcasted_iota(jnp.int32, (DCH, 128), 0) == lax.broadcasted_iota(jnp.int32, (DCH, 128), 1), 1.0, 0.0
    ).astype(BF16)
    for number in range(4):
        held = f_buf[128 * number : 128 * number + 128, :]
        ordered = jnp.concatenate(
            [held[32 * xx + 16 * part : 32 * xx + 16 * part + 16] for part in range(2) for xx in range(4)],
            axis=0,
        )
        e_send[number] = dot_nt(some_rows, ordered).astype(BF16)
        away = end_of(number) != c

        @pl.when(away)
        def _():
            e_copy(number).start()

        @pl.when(jnp.logical_not(away))
        def _():
            e_buf[
                pl.ds(pl.multiple_of((chunk_of(z, number) % 2) * DCH, DCH), DCH),
                pl.ds(pl.multiple_of(h * 128, 128), 128),
            ] = e_send[number]

    pltpu.make_async_copy(m_buf.at[pl.ds(0, 15)], m_buf.at[pl.ds(0, 15)], a_rs.at[2]).wait()
    top = jnp.max(m_buf[...], axis=0)
    for j in range(2):
        for k in range(2):
            q = 2 * j + k
            scale = jnp.max(top[q : q + 1, :])
            ds_out[j, k] = scale
            dc_out[:, j, k, :] = (nd_out[:, j, k, :] / (scale + scale_eps)).astype(BF16)

    pltpu.make_async_copy(
        hs_buf.at[pl.ds(0, 15 * CAP), :], hs_buf.at[pl.ds(0, 15 * CAP), :], a_rs.at[1]
    ).wait()
    gg_out[...] = (slope[...] * hs_buf[...].astype(F32)).astype(BF16)

    for number in range(4):
        other = start_of(number)

        @pl.when(other != c)
        def _():
            block = e_buf.at[
                pl.ds((number // 2) * DCH, DCH), pl.ds((number % 2) * 128, 128)
            ]
            pltpu.make_async_copy(block, block, e_rs.at[number]).wait()

    ig_out[...] = e_buf[...]

    for links in (
        codes_ring.links, x_links, dy_ring.links, dx_ring.links, g_ring.links,
        q_ring.links, r_ring.links, h_ring.links, s_links,
    ):
        links.drain()
    for number, (hops, first, change, steps) in enumerate(streams):
        for step in range(steps):
            ring_copy(number, step).wait_send()
    for number in range(2):
        pltpu.make_async_copy(
            u_buf.at[pl.ds(0, 15 * CAP), :], u_buf.at[pl.ds(0, 15 * CAP), :], a_ss.at[number]
        ).wait()
    pltpu.make_async_copy(m_buf.at[pl.ds(0, 15)], m_buf.at[pl.ds(0, 15)], a_ss.at[2]).wait()
    pltpu.make_async_copy(
        f_buf.at[pl.ds(0, 480), :], f_buf.at[pl.ds(0, 480), :], a_ss.at[3]
    ).wait()
    for number in range(4):

        @pl.when(end_of(number) != c)
        def _():
            e_copy(number).wait_send()


def settle(*refs):
    for held, out in zip(refs[:6], refs[7:13]):
        out[...] = held[...]
    for j in range(2):
        for k in range(2):
            refs[13][j, k] = refs[6][j, k]


def per_device(
    rollout, lengths, route, up_codes, up_scales, block_rows, delta, adam_m, adam_v, gate_pre, hidden_grad
):
    vmem = pl.BlockSpec(memory_space=pltpu.VMEM)
    smem = pl.BlockSpec(memory_space=pltpu.SMEM)
    dma = pltpu.SemaphoreType.DMA

    def bf(*shape):
        return pltpu.VMEM(shape, BF16)

    def fl(*shape):
        return pltpu.VMEM(shape, F32)

    smem_of = pltpu.SMEM
    block4 = delta.shape
    scratch = [
        smem_of((2,), jnp.int32), smem_of((2, 20), F32), smem_of((2, 2), jnp.int32),
        bf(ROWS, D), pltpu.VMEM((1, ROWS), jnp.int32), fl(*block4), fl(*block4), fl(*block4),
        bf(256, COLS), bf(256, COLS),
        bf(256, COLS), bf(256, COLS), fl(256, COLS), bf(KS, COLS), bf(KS, COLS), bf(4 * ROWS, KS),
        bf(256, 1024), bf(4, GB, COLS), bf(4 * ROWS, COLS),
        bf(4 * ROWS, COLS), bf(2, 64, COLS), bf(2, 64, COLS), bf(2, ROWS, COLS),
        bf(256, COLS), bf(256, COLS),
        bf(256, 1024), bf(2, 32, 1024), bf(2, 32, 1024), bf(2, 64, 1024),
        bf(64, 1024), bf(2, 16, 512), bf(2, 16, 512), bf(2, 16, 1024),
        fl(8, 128), fl(NT, 8, 128), fl(KS, 256), bf(KS, 256), bf(KS, 256),
        bf(4, 4, DCH, 256), bf(4, 4, DCH, 256), bf(512, 128), bf(512, 128), bf(4, DCH, 128), bf(160, 256),
        bf(4, ROWS, BLK), bf(512, 256),
        dma((11,)),
        dma((6,)), dma((6,)), dma((6,)), dma((6,)), dma((6,)), dma((6,)), dma((6,)), dma((6,)),
        dma((6,)), dma((6,)), dma((6,)), dma((6,)), dma((6,)), dma((6,)), dma((6,)), dma((6,)),
        dma((4,)), dma((4,)), dma((16,)), dma((16,)), dma((4,)), dma((4,)), dma((4,)), dma((4,)),
    ]
    block = jax.ShapeDtypeStruct(delta.shape, F32)
    outs = pl.pallas_call(
        kernel,
        out_shape=(
            jax.ShapeDtypeStruct((160, 256), BF16),
            jax.ShapeDtypeStruct((256, COLS), BF16),
            block,
            block,
            block,
            jax.ShapeDtypeStruct((2, 2), F32),
            jax.ShapeDtypeStruct(delta.shape, BF16),
        ),
        in_specs=[pl.BlockSpec(memory_space=pl.ANY)] * 11,
        out_specs=(vmem, vmem, vmem, vmem, vmem, smem, vmem),
        scratch_shapes=scratch,
        compiler_params=pltpu.CompilerParams(
            collective_id=0, has_side_effects=True, vmem_limit_bytes=VLIM * 1024 * 1024
        ),
        cost_estimate=pl.CostEstimate(flops=3 * 10**9, bytes_accessed=4 * 10**6, transcendentals=0),
    )(
        lengths, up_scales.T, block_rows, rollout, route.T, up_codes, delta, adam_m, adam_v, gate_pre, hidden_grad
    )
    large = outs[:5] + outs[6:]
    shapes = tuple(jax.ShapeDtypeStruct(held.shape, held.dtype) for held in large)
    results = pl.pallas_call(
        settle,
        out_shape=shapes + (jax.ShapeDtypeStruct((2, 2), F32),),
        in_specs=[vmem] * 6 + [smem],
        out_specs=(vmem,) * 6 + (smem,),
        compiler_params=pltpu.CompilerParams(vmem_limit_bytes=VLIM2 * 1024 * 1024),
    )(*large, outs[5])
    return (results[0].T,) + tuple(results[1:5]) + (results[6], results[5])


def solution(mesh):
    placed = (
        P("tok", None),
        P("tok"),
        P("tok", None),
        P("tok", "col"),
        P(None, "col"),
        P("col", None),
        P("tok", "col", None, None),
        P("tok", "col", None, None),
        P("tok", "col", None, None),
        P("tok", "col"),
        P("tok", "col"),
    )
    return jax.shard_map(
        per_device,
        mesh=mesh,
        in_specs=placed,
        out_specs=(
            P("tok", "col"),
            P("tok", "col"),
            P("tok", "col", None, None),
            P("tok", "col", None, None),
            P("tok", "col", None, None),
            P("col", None),
            P("tok", "col", None, None),
        ),
        check_vma=False,
    )
```

```python
import functools

import jax
import jax.numpy as jnp
from jax import lax
from jax.experimental import pallas as pl
from jax.experimental.pallas import tpu as pltpu
from jax.sharding import PartitionSpec as P

BLK = 256
VLIM = 62
VLIM2 = 62
RESP = 64
STEP = 1000
D = 5120
NT = 16
NZ = 16
CAP = 16
ROWS = 128
COLS = 512
KS = D // 4
CROWS = 320
DCH = KS // NZ
GB = 144

beta_first = 0.9
beta_second = 0.999
step_rate = 0.01
adam_eps = 1e-08
scale_eps = 1e-06

MESH = pl.DeviceIdType.MESH
F32 = jnp.float32
BF16 = jnp.bfloat16


def dot_nn(a, b):
    return lax.dot_general(a, b, (((1,), (0,)), ((), ())), preferred_element_type=F32)


def dot_nt(a, b):
    return lax.dot_general(a, b, (((1,), (1,)), ((), ())), preferred_element_type=F32)


def dot_tn(a, b):
    return lax.dot_general(a, b, (((0,), (0,)), ((), ())), preferred_element_type=F32)


def is_same(a, b):
    return (1 - jnp.minimum(jnp.abs(a - b), 1)).astype(F32)


class Links:
    def __init__(self, send, recv):
        self.send, self.recv = send, recv
        self.sent = []

    def copy(self, src, dst, number, tok, col):
        return pltpu.make_async_remote_copy(
            src_ref=src,
            dst_ref=dst,
            send_sem=self.send.at[number],
            recv_sem=self.recv.at[number],
            device_id={"tok": tok, "col": col},
            device_id_type=MESH,
        )

    def start(self, src, dst, number, tok, col):
        made = self.copy(src, dst, number, tok, col)
        made.start()
        self.sent.append(made)

    def wait(self, dst, number):
        pltpu.make_async_copy(dst, dst, self.recv.at[number]).wait()

    def drain(self):
        for made in self.sent:
            made.wait_send()


class RingGather:
    def __init__(self, links, me, device, block, half):
        self.links, self.block, self.half, self.device = links, block, half, device
        self.me = me
        self.right, self.left, self.far = (me + 1) % 4, (me + 3) % 4, (me + 2) % 4

    def put(self, src, index, part, number, to):
        self.links.start(self.half(src, part), self.half(self.block(index), part), number, *self.device(to))

    def got(self, index, part, number):
        self.links.wait(self.half(self.block(index), part), number)

    def begin(self, src):
        self.begin_far(src)
        self.begin_near(src)

    def begin_far(self, src):
        self.put(src, self.me, 0, 0, self.right)
        self.put(src, self.me, 1, 1, self.left)

    def begin_near(self, src):
        self.put(src, self.me, 1, 2, self.right)
        self.put(src, self.me, 0, 3, self.left)

    def forward(self):
        self.got(self.left, 0, 0)
        self.put(self.block(self.left), self.left, 0, 4, self.right)
        self.got(self.right, 1, 1)
        self.put(self.block(self.right), self.right, 1, 5, self.left)

    def finish(self):
        self.got(self.left, 1, 2)
        self.got(self.right, 0, 3)
        self.got(self.far, 0, 4)
        self.got(self.far, 1, 5)


class DirectGather:
    def __init__(self, links, me, device, block):
        self.links, self.me, self.device, self.block = links, me, device, block

    def begin(self):
        for step in (1, 3, 2):
            own = self.block(self.me)
            self.links.start(own, own, step - 1, *self.device((self.me + step) % 4))

    def finish(self):
        for step in (1, 3, 2):
            self.links.wait(self.block((self.me + 4 - step) % 4), step - 1)


class RingReduce:
    def __init__(self, links, me, device, part, half, first, stage, second):
        self.links, self.part, self.half, self.device = links, part, half, device
        self.first, self.stage, self.second = first, stage, second
        self.me = me
        self.right, self.left, self.far = (me + 1) % 4, (me + 3) % 4, (me + 2) % 4

    def put(self, src, dst, number, to):
        self.links.start(src, dst, number, *self.device(to))

    def begin(self):
        self.put(self.half(self.part(self.far), 0), self.first.at[0], 0, self.right)
        self.put(self.half(self.part(self.far), 1), self.first.at[1], 1, self.left)
        self.put(self.half(self.part(self.right), 1), self.half(self.second.at[0], 1), 2, self.right)
        self.put(self.half(self.part(self.left), 0), self.half(self.second.at[1], 0), 3, self.left)

    def forward(self):
        self.links.wait(self.first.at[0], 0)
        self.stage[0] = (
            self.half(self.part(self.right), 0)[...].astype(F32) + self.first[0].astype(F32)
        ).astype(BF16)
        self.put(self.stage.at[0], self.half(self.second.at[0], 0), 4, self.right)
        self.links.wait(self.first.at[1], 1)
        self.stage[1] = (
            self.half(self.part(self.left), 1)[...].astype(F32) + self.first[1].astype(F32)
        ).astype(BF16)
        self.put(self.stage.at[1], self.half(self.second.at[1], 1), 5, self.left)

    def finish(self):
        self.links.wait(self.half(self.second.at[0], 1), 2)
        self.links.wait(self.half(self.second.at[1], 0), 3)
        self.links.wait(self.half(self.second.at[0], 0), 4)
        self.links.wait(self.half(self.second.at[1], 1), 5)

    def total(self, own):
        return own + (self.second[0].astype(F32) + self.second[1].astype(F32))


def rows_half(size):
    def half(ref, part):
        return ref.at[pl.ds(part * size, size), :]

    return half


def lanes_half(size):
    def half(ref, part):
        return ref.at[:, pl.ds(part * size, size)]

    return half


def g_half(ref, part):
    return ref.at[pl.ds(0, 64), :] if part == 0 else ref.at[pl.ds(64, GB - 64), :]


def kernel(
    lengths_h, scales_h, brows_h, rollout_h, route_h, codes_h, delta_h, m_h, v_h, gate_h, hidden_h,
    ig_out, gg_out, nd_out, nm_out, nv_out, ds_out, dc_out,
    lengths, scales, brows, rollout, route, delta, adam_m, adam_v, gate_pre, hidden_grad,
    u_send, u_buf, slope, w_buf, w_eff, x_buf, d_buf, g_buf, g_all,
    h_part, h_first, h_stage, h_second, hs_send, hs_buf,
    q_part, q_first, q_stage, q_second, r_part, r_first, r_stage, r_second,
    m_send, m_buf, z_own, z_give, z_take, z_send, z_recv, f_send, f_buf, e_send, e_buf, chosen_rows, put_both,
    in_s, c_ss, c_rs, dy_ss, dy_rs, dx_ss, dx_rs, g_ss, g_rs, x_ss, x_rs, h_ss, h_rs,
    q_ss, q_rs, r_ss, r_rs, s_ss, s_rs, z_ss, z_rs, a_ss, a_rs, e_ss, e_rs,
):
    t = lax.axis_index("tok")
    c = lax.axis_index("col")
    y, x = t // 4, t % 4
    z, h = c // 2, c % 2
    sibling = 2 * z + 1 - h

    def at_x(other):
        return y * 4 + other, c

    def at_y(other):
        return other * 4 + x, c

    own_codes = w_buf.at[pl.ds(x * CROWS, CROWS), :]
    pairs = (
        (hidden_h, hidden_grad), (gate_h, gate_pre), (delta_h, delta), (codes_h, own_codes),
        (route_h, route), (lengths_h, lengths), (rollout_h, rollout), (brows_h, brows),
        (scales_h, scales), (m_h, adam_m), (v_h, adam_v),
    )
    loads = [pltpu.make_async_copy(src, dst, in_s.at[i]) for i, (src, dst) in enumerate(pairs)]
    for load in loads[:4]:
        load.start()

    def chunk_of(chip, row):
        return (chip + 22 - 4 * row) % NZ

    def end_of(row):
        chunk = chunk_of(z, row)
        return 2 * (4 * row + chunk // 4) + (chunk // 2) % 2

    def start_of(number):
        row = z // 4
        chunk = 4 * (z % 4) + 2 * h + number // 2
        return 2 * ((chunk + 10 + 4 * row) % NZ) + number % 2

    barrier = pltpu.get_barrier_semaphore()

    def greet(tok, col):
        pl.semaphore_signal(barrier, inc=1, device_id={"tok": tok, "col": col}, device_id_type=MESH)

    def greet_plane(i, carry):
        greet((t + i) % NT, c)
        return carry

    lax.fori_loop(1, NT, greet_plane, 0)
    greet(t, sibling)
    for distance in (1, 2, NZ - 2, NZ - 1):
        greet(t, 2 * ((z + distance) % NZ) + h)
    for number in range(4):
        for other in (end_of(number), start_of(number)):

            @pl.when(other != c)
            def _():
                greet(t, other)

    for load in loads[4:]:
        load.start()
    stays = end_of(z // 4) == c

    loads[0].wait()
    loads[1].wait()

    def gate_rows(i, carry):
        at = pl.ds(pl.multiple_of(i * 32, 32), 32)
        v = gate_pre[at, :].astype(F32)
        hg = hidden_grad[at, :].astype(F32)
        s = 1.0 / (1.0 + jnp.exp(-v))
        slope[at, :] = hg * (s * (1.0 + v * (1.0 - s)))
        u_send[at, :] = (hg * (v * s)).astype(BF16)
        return carry

    lax.fori_loop(0, 8, gate_rows, 0)

    dx_ring = DirectGather(
        Links(dx_ss, dx_rs), x, at_x, lambda i: d_buf.at[pl.ds(y * 64 + i * 16, 16), :]
    )
    own_delta = dx_ring.block(x)
    loads[2].wait()
    for j in range(2):
        for k in range(2):
            own_delta[:, (2 * j + k) * BLK : (2 * j + k + 1) * BLK] = delta[:, j, k, :].astype(BF16)
    loads[3].wait()

    pl.semaphore_wait(barrier, jnp.where(stays, 26, 28))

    dx_ring.begin()

    def a2a_copy(src, dst, number, other):
        return pltpu.make_async_remote_copy(
            src_ref=src.at[pl.ds(pl.multiple_of(other * CAP, CAP), CAP), :],
            dst_ref=dst.at[pl.ds(pl.multiple_of(t * CAP, CAP), CAP), :],
            send_sem=a_ss.at[number],
            recv_sem=a_rs.at[number],
            device_id={"tok": other, "col": c},
            device_id_type=MESH,
        )

    def u_step(i, carry):
        a2a_copy(u_send, u_buf, 0, (t + i) % NT).start()
        return carry

    lax.fori_loop(1, NT, u_step, 0)
    own_cap = pl.ds(pl.multiple_of(t * CAP, CAP), CAP)
    u_buf[own_cap, :] = u_send[own_cap, :]

    codes_ring = RingGather(
        Links(c_ss, c_rs), x, at_x, lambda i: w_buf.at[pl.ds(i * CROWS, CROWS), :], rows_half(CROWS // 2)
    )
    codes_ring.begin_far(own_codes)

    for load in loads[4:]:
        load.wait()
    lane = lax.broadcasted_iota(jnp.int32, (ROWS, ROWS), 1)
    row = lax.broadcasted_iota(jnp.int32, (ROWS, ROWS), 0)
    eye = jnp.where(lane == row, 1.0, 0.0).astype(BF16)
    route_rows = jnp.broadcast_to(route[...].astype(F32), (ROWS, ROWS)).astype(BF16)
    goes = dot_nt(eye, route_rows)
    onehot = jnp.where(goes == lane.astype(F32), 1.0, 0.0)
    lower = jnp.where(lane < row, 1.0, 0.0)
    earlier = dot_nn(lower.astype(BF16), onehot.astype(BF16))
    slot = jnp.sum(earlier * onehot, axis=1, keepdims=True)
    target = goes * CAP + slot
    target_row = dot_tn(target.astype(BF16), eye)
    wide = lax.broadcasted_iota(jnp.int32, (ROWS, NT * CAP), 1).astype(F32)
    pick = jnp.where(wide == target[:, 0:1], 1.0, 0.0).astype(BF16)
    slot_row = lax.broadcasted_iota(jnp.int32, (NT * CAP, ROWS), 0).astype(F32)
    put_slots = jnp.where(slot_row == target_row[0:1, :], 1.0, 0.0).astype(BF16)
    row_id = lax.broadcasted_iota(jnp.int32, (ROWS, 1), 0)
    live = jnp.where(row_id < RESP, lengths[0], lengths[1])
    row_weight = jnp.where(row_id % RESP < live, RESP / live.astype(F32), 0.0)

    dx_ring.finish()
    dy_ring = RingGather(
        Links(dy_ss, dy_rs), y, at_y, lambda i: d_buf.at[pl.ds(i * 64, 64), :], rows_half(32)
    )
    dy_ring.begin(dy_ring.block(y))

    pltpu.make_async_copy(
        u_buf.at[pl.ds(0, 15 * CAP), :], u_buf.at[pl.ds(0, 15 * CAP), :], a_rs.at[0]
    ).wait()
    up_grad = (row_weight * dot_nn(pick, u_buf[...])).astype(BF16)
    g_ring = RingGather(Links(g_ss, g_rs), y, at_y, lambda i: g_buf.at[i], g_half)
    own_g = g_buf.at[y]
    own_g[0:ROWS, :] = up_grad
    own_g[ROWS:GB, :] = jnp.concatenate([target_row[0 : GB - ROWS, :]] * 4, axis=1).astype(BF16)
    g_ring.begin(own_g)
    codes_ring.begin_near(own_codes)

    codes_ring.forward()
    dy_ring.forward()
    g_ring.forward()

    def choose_rows(i, carry):
        at = pl.ds(pl.multiple_of(i * 32, 32), 32)
        picked = [jnp.zeros((32, BLK), BF16)] * 4
        for block in range(D // BLK):
            held = rollout[at, block * BLK : (block + 1) * BLK]
            for q in range(4):
                on = jnp.full((32, BLK), is_same(brows[q // 2, q % 2], block), F32).astype(BF16)
                picked[q] = picked[q] + on * held
        for q in range(4):
            chosen_rows[q, at, :] = picked[q]
        return carry

    lax.fori_loop(0, 4, choose_rows, 0)
    for j in range(2):
        for k in range(2):
            chosen = chosen_rows[2 * j + k]
            grad = dot_tn(chosen, up_grad[:, j * BLK : (j + 1) * BLK]).astype(BF16)
            for yy in range(4):
                for xx in range(4):
                    q_part[
                        64 * xx + 16 * yy : 64 * xx + 16 * yy + 16,
                        (2 * j + k) * BLK : (2 * j + k + 1) * BLK,
                    ] = grad[64 * yy + 16 * xx : 64 * yy + 16 * xx + 16, :]
    q_ring = RingReduce(
        Links(q_ss, q_rs), x, at_x, lambda i: q_part.at[pl.ds(i * 64, 64), :], rows_half(32),
        q_first, q_stage, q_second,
    )
    x_buf[pl.ds(y * ROWS, ROWS), :] = rollout[:, pl.ds(pl.multiple_of(y * KS, KS), KS)]

    dy_ring.finish()
    g_ring.finish()
    for yy in range(4):
        g_all[ROWS * yy : ROWS * (yy + 1), :] = g_buf[yy, 0:ROWS, :]

    x_links = Links(x_ss, x_rs)
    for step in (1, 3, 2):
        to = (y + step) % 4
        x_links.start(
            rollout.at[pl.ds(64 * h, 64), pl.ds(pl.multiple_of(to * KS, KS), KS)],
            x_buf.at[pl.ds(y * ROWS + 64 * h, 64), :],
            step - 1,
            *at_y(to),
        )


    def weight_rows(index, carry):
        block = y * 5 + index // 4
        part = index % 4
        for j in range(2):
            scale = scales[j, block]
            on = [is_same(brows[j, k], block) for k in range(2)]
            at = pl.ds(pl.multiple_of(index * 64, 64), 64)
            held = pl.ds(pl.multiple_of(64 * part, 64), 64)
            value = w_buf[at, j * BLK : (j + 1) * BLK].astype(F32) * scale
            for k in range(2):
                q = 2 * j + k
                value = value + on[k] * d_buf[held, q * BLK : (q + 1) * BLK].astype(F32)
            w_eff[at, j * BLK : (j + 1) * BLK] = value.astype(BF16)
        return carry

    s_links = Links(s_ss, s_rs)
    give_rows = pl.ds(pl.multiple_of(256 * (1 - h), 256), 256)
    keep_rows = pl.ds(pl.multiple_of(256 * h, 256), 256)
    for order, part in enumerate((x, codes_ring.left, codes_ring.right, codes_ring.far)):
        if order == 1:
            codes_ring.got(part, 1, 2)
        if order == 2:
            codes_ring.got(part, 0, 3)
        if order == 3:
            codes_ring.got(part, 0, 4)
            codes_ring.got(part, 1, 5)
            q_ring.begin()
        lax.fori_loop(5 * part, 5 * part + 5, weight_rows, 0)
        at = pl.ds(pl.multiple_of(part * CROWS, CROWS), CROWS)
        z_give[at, :] = dot_nt(w_eff[at, :], g_all[give_rows, :]).astype(BF16)
        s_links.start(z_give.at[at, :], z_take.at[at, :], order, t, sibling)
        z_own[at, :] = dot_nt(w_eff[at, :], g_all[keep_rows, :])

    wanted = jnp.concatenate(
        [g_buf[2 * h + half, ROWS : ROWS + 16, 0:128].astype(F32)[0:1, :] for half in range(2)], axis=1
    )
    spot = lax.broadcasted_iota(jnp.int32, (2 * NT * CAP, 256), 0)
    side = lax.broadcasted_iota(jnp.int32, (2 * NT * CAP, 256), 1) // 128
    slot_of = ((spot // 32) * 16 + spot % 16).astype(F32)
    put_both[...] = jnp.where((slot_of == wanted) & (side == (spot // 16) % 2), 1.0, 0.0).astype(BF16)

    for order, part in enumerate((x, codes_ring.left, codes_ring.right, codes_ring.far)):
        s_links.wait(z_take.at[pl.ds(pl.multiple_of(part * CROWS, CROWS), CROWS), :], order)

    def own_chunk(chip):
        at = pl.ds(pl.multiple_of(chunk_of(chip, y) * DCH, DCH), DCH)
        return z_own[at, :] + z_take[at, :].astype(F32)

    streams = ((2, 8, NZ - 2, 4), (NZ - 2, NZ - 6, 2, 3), (1, 7, NZ - 2, 4), (NZ - 1, NZ - 7, 2, 4))

    def ring_copy(number, step):
        return pltpu.make_async_remote_copy(
            src_ref=z_send.at[number, step],
            dst_ref=z_recv.at[number, step],
            send_sem=z_ss.at[number * 4 + step],
            recv_sem=z_rs.at[number * 4 + step],
            device_id={"tok": t, "col": 2 * ((z + streams[number][0]) % NZ) + h},
            device_id_type=MESH,
        )

    def ring_send(number, step, *joins):
        hops, first, change, steps = streams[number]
        value = own_chunk((z + first + step * change) % NZ)
        for stream, index in joins:
            ring_copy(stream, index).wait_recv()
            value = value + z_recv[stream, index].astype(F32)
        z_send[number, step] = value.astype(BF16)
        ring_copy(number, step).start()

    def ring_step(step):
        if step == 0:
            ring_send(0, 0)
            ring_send(3, 0)
            ring_send(2, 0)
            ring_send(3, 1)
            ring_send(2, 1)
            ring_send(1, 0, (3, 0))
        else:
            ring_send(0, step, (2, step - 1), (0, step - 1))
            if step < 3:
                ring_send(1, step, (3, step), (1, step - 1))
                ring_send(3, step + 1)
                ring_send(2, step + 1)

    ring_step(0)
    q_ring.forward()
    for step in (1, 3, 2):
        source = (y + 4 - step) % 4
        mine = x_buf.at[pl.ds(source * ROWS + 64 * h, 64), :]
        x_links.wait(mine, step - 1)
        x_links.start(mine, mine, 3 + step - 1, t, sibling)
    ring_step(1)
    q_ring.finish()
    r_part[...] = q_ring.total(q_part[pl.ds(x * 64, 64), :].astype(F32)).astype(BF16)
    r_ring = RingReduce(
        Links(r_ss, r_rs), y, at_y, lambda i: r_part.at[pl.ds(i * 16, 16), :], lanes_half(512),
        r_first, r_stage, r_second,
    )
    r_ring.begin()
    ring_step(2)

    for step in (1, 3, 2):
        source = (y + 4 - step) % 4
        x_links.wait(x_buf.at[pl.ds(source * ROWS + 64 * (1 - h), 64), :], 3 + step - 1)

    def up_rows(i, carry):
        at = pl.ds(pl.multiple_of(i * ROWS, ROWS), ROWS)
        h_part[at, :] = dot_nn(x_buf[at, :], w_eff[...]).astype(BF16)
        return carry

    lax.fori_loop(0, 4, up_rows, 0)
    h_ring = RingReduce(
        Links(h_ss, h_rs), y, at_y, lambda i: h_part.at[pl.ds(i * ROWS, ROWS), :], rows_half(64),
        h_first, h_stage, h_second,
    )
    h_ring.begin()
    r_ring.forward()
    ring_step(3)
    total = own_chunk(z)
    for number, (hops, first, change, steps) in enumerate(streams):
        ring_copy(number, steps - 1).wait_recv()
        total = total + z_recv[number, steps - 1].astype(F32)
    chunk = jnp.concatenate([total.astype(BF16), jnp.zeros((128 - DCH, 256), BF16)], axis=0)
    f_send[...] = dot_nt(put_both[...], chunk).astype(BF16)

    def f_copy(other):
        return pltpu.make_async_remote_copy(
            src_ref=f_send.at[pl.ds(pl.multiple_of(other * 32, 32), 32), :],
            dst_ref=f_buf.at[pl.ds(pl.multiple_of(t * 32, 32), 32), :],
            send_sem=a_ss.at[3],
            recv_sem=a_rs.at[3],
            device_id={"tok": other, "col": c},
            device_id_type=MESH,
        )

    def f_step(i, carry):
        f_copy((t + i) % NT).start()
        return carry

    lax.fori_loop(1, NT, f_step, 0)
    own_f = pl.ds(pl.multiple_of(t * 32, 32), 32)
    f_buf[own_f, :] = f_send[own_f, :]

    h_ring.forward()
    r_ring.finish()
    gradient = r_ring.total(r_part[pl.ds(pl.multiple_of(y * 16, 16), 16), :].astype(F32))

    tops = []
    for j in range(2):
        for k in range(2):
            q = 2 * j + k
            g = gradient[:, q * BLK : (q + 1) * BLK]
            new_m = beta_first * adam_m[:, j, k, :] + (1.0 - beta_first) * g
            new_v = beta_second * adam_v[:, j, k, :] + (1.0 - beta_second) * g * g
            corrected_m = new_m / (1.0 - beta_first**STEP)
            corrected_v = new_v / (1.0 - beta_second**STEP)
            new_delta = delta[:, j, k, :] - step_rate * corrected_m / (
                jnp.sqrt(corrected_v) + adam_eps
            )
            nm_out[:, j, k, :] = new_m
            nv_out[:, j, k, :] = new_v
            nd_out[:, j, k, :] = new_delta
            tops.append(jnp.max(jnp.abs(new_delta)))
    tile_row = lax.broadcasted_iota(jnp.int32, (8, 128), 0)
    tile = jnp.zeros((8, 128), F32)
    for q in range(4):
        tile = jnp.where(tile_row == q, tops[q], tile)
    m_send[...] = tile
    m_buf[t] = tile

    def m_copy(other):
        return pltpu.make_async_remote_copy(
            src_ref=m_send,
            dst_ref=m_buf.at[t],
            send_sem=a_ss.at[2],
            recv_sem=a_rs.at[2],
            device_id={"tok": other, "col": c},
            device_id_type=MESH,
        )

    def m_step(i, carry):
        m_copy((t + i) % NT).start()
        return carry

    lax.fori_loop(1, NT, m_step, 0)

    h_ring.finish()
    up_value = h_ring.total(h_part[pl.ds(y * ROWS, ROWS), :].astype(F32)) * row_weight
    hs_send[...] = dot_nn(put_slots, up_value.astype(BF16)).astype(BF16)

    def h_step(i, carry):
        a2a_copy(hs_send, hs_buf, 1, (t + i) % NT).start()
        return carry

    lax.fori_loop(1, NT, h_step, 0)
    hs_buf[own_cap, :] = hs_send[own_cap, :]

    pltpu.make_async_copy(
        f_buf.at[pl.ds(0, 480), :], f_buf.at[pl.ds(0, 480), :], a_rs.at[3]
    ).wait()

    def e_copy(number):
        chunk_here = chunk_of(z, number)
        return pltpu.make_async_remote_copy(
            src_ref=e_send.at[number],
            dst_ref=e_buf.at[pl.ds((chunk_here % 2) * DCH, DCH), pl.ds(pl.multiple_of(h * 128, 128), 128)],
            send_sem=e_ss.at[number],
            recv_sem=e_rs.at[(chunk_here % 2) * 2 + h],
            device_id={"tok": t, "col": end_of(number)},
            device_id_type=MESH,
        )

    some_rows = jnp.where(
        lax.broadcasted_iota(jnp.int32, (DCH, 128), 0) == lax.broadcasted_iota(jnp.int32, (DCH, 128), 1), 1.0, 0.0
    ).astype(BF16)
    for number in range(4):
        held = f_buf[128 * number : 128 * number + 128, :]
        ordered = jnp.concatenate(
            [held[32 * xx + 16 * part : 32 * xx + 16 * part + 16] for part in range(2) for xx in range(4)],
            axis=0,
        )
        e_send[number] = dot_nt(some_rows, ordered).astype(BF16)
        away = end_of(number) != c

        @pl.when(away)
        def _():
            e_copy(number).start()

        @pl.when(jnp.logical_not(away))
        def _():
            e_buf[
                pl.ds(pl.multiple_of((chunk_of(z, number) % 2) * DCH, DCH), DCH),
                pl.ds(pl.multiple_of(h * 128, 128), 128),
            ] = e_send[number]

    pltpu.make_async_copy(m_buf.at[pl.ds(0, 15)], m_buf.at[pl.ds(0, 15)], a_rs.at[2]).wait()
    top = jnp.max(m_buf[...], axis=0)
    for j in range(2):
        for k in range(2):
            q = 2 * j + k
            scale = jnp.max(top[q : q + 1, :])
            ds_out[j, k] = scale
            dc_out[:, j, k, :] = (nd_out[:, j, k, :] / (scale + scale_eps)).astype(BF16)

    pltpu.make_async_copy(
        hs_buf.at[pl.ds(0, 15 * CAP), :], hs_buf.at[pl.ds(0, 15 * CAP), :], a_rs.at[1]
    ).wait()
    gg_out[...] = (slope[...] * hs_buf[...].astype(F32)).astype(BF16)

    for number in range(4):
        other = start_of(number)

        @pl.when(other != c)
        def _():
            block = e_buf.at[
                pl.ds((number // 2) * DCH, DCH), pl.ds((number % 2) * 128, 128)
            ]
            pltpu.make_async_copy(block, block, e_rs.at[number]).wait()

    ig_out[...] = e_buf[...]

    for links in (
        codes_ring.links, x_links, dy_ring.links, dx_ring.links, g_ring.links,
        q_ring.links, r_ring.links, h_ring.links, s_links,
    ):
        links.drain()
    for number, (hops, first, change, steps) in enumerate(streams):
        for step in range(steps):
            ring_copy(number, step).wait_send()
    for number in range(2):
        pltpu.make_async_copy(
            u_buf.at[pl.ds(0, 15 * CAP), :], u_buf.at[pl.ds(0, 15 * CAP), :], a_ss.at[number]
        ).wait()
    pltpu.make_async_copy(m_buf.at[pl.ds(0, 15)], m_buf.at[pl.ds(0, 15)], a_ss.at[2]).wait()
    pltpu.make_async_copy(
        f_buf.at[pl.ds(0, 480), :], f_buf.at[pl.ds(0, 480), :], a_ss.at[3]
    ).wait()
    for number in range(4):

        @pl.when(end_of(number) != c)
        def _():
            e_copy(number).wait_send()


def settle(*refs):
    for held, out in zip(refs[:6], refs[7:13]):
        out[...] = held[...]
    for j in range(2):
        for k in range(2):
            refs[13][j, k] = refs[6][j, k]


def per_device(
    rollout, lengths, route, up_codes, up_scales, block_rows, delta, adam_m, adam_v, gate_pre, hidden_grad
):
    vmem = pl.BlockSpec(memory_space=pltpu.VMEM)
    smem = pl.BlockSpec(memory_space=pltpu.SMEM)
    dma = pltpu.SemaphoreType.DMA

    def bf(*shape):
        return pltpu.VMEM(shape, BF16)

    def fl(*shape):
        return pltpu.VMEM(shape, F32)

    smem_of = pltpu.SMEM
    block4 = delta.shape
    scratch = [
        smem_of((2,), jnp.int32), smem_of((2, 20), F32), smem_of((2, 2), jnp.int32),
        bf(ROWS, D), pltpu.VMEM((1, ROWS), jnp.int32), fl(*block4), fl(*block4), fl(*block4),
        bf(256, COLS), bf(256, COLS),
        bf(256, COLS), bf(256, COLS), fl(256, COLS), bf(KS, COLS), bf(KS, COLS), bf(4 * ROWS, KS),
        bf(256, 1024), bf(4, GB, COLS), bf(4 * ROWS, COLS),
        bf(4 * ROWS, COLS), bf(2, 64, COLS), bf(2, 64, COLS), bf(2, ROWS, COLS),
        bf(256, COLS), bf(256, COLS),
        bf(256, 1024), bf(2, 32, 1024), bf(2, 32, 1024), bf(2, 64, 1024),
        bf(64, 1024), bf(2, 16, 512), bf(2, 16, 512), bf(2, 16, 1024),
        fl(8, 128), fl(NT, 8, 128), fl(KS, 256), bf(KS, 256), bf(KS, 256),
        bf(4, 4, DCH, 256), bf(4, 4, DCH, 256), bf(512, 128), bf(512, 128), bf(4, DCH, 128), bf(160, 256),
        bf(4, ROWS, BLK), bf(512, 256),
        dma((11,)),
        dma((6,)), dma((6,)), dma((6,)), dma((6,)), dma((6,)), dma((6,)), dma((6,)), dma((6,)),
        dma((6,)), dma((6,)), dma((6,)), dma((6,)), dma((6,)), dma((6,)), dma((6,)), dma((6,)),
        dma((4,)), dma((4,)), dma((16,)), dma((16,)), dma((4,)), dma((4,)), dma((4,)), dma((4,)),
    ]
    block = jax.ShapeDtypeStruct(delta.shape, F32)
    outs = pl.pallas_call(
        kernel,
        out_shape=(
            jax.ShapeDtypeStruct((160, 256), BF16),
            jax.ShapeDtypeStruct((256, COLS), BF16),
            block,
            block,
            block,
            jax.ShapeDtypeStruct((2, 2), F32),
            jax.ShapeDtypeStruct(delta.shape, BF16),
        ),
        in_specs=[pl.BlockSpec(memory_space=pl.ANY)] * 11,
        out_specs=(vmem, vmem, vmem, vmem, vmem, smem, vmem),
        scratch_shapes=scratch,
        compiler_params=pltpu.CompilerParams(
            collective_id=0, has_side_effects=True, vmem_limit_bytes=VLIM * 1024 * 1024
        ),
        cost_estimate=pl.CostEstimate(flops=3 * 10**9, bytes_accessed=4 * 10**6, transcendentals=0),
    )(
        lengths, up_scales.T, block_rows, rollout, route.T, up_codes, delta, adam_m, adam_v, gate_pre, hidden_grad
    )
    large = outs[:5] + outs[6:]
    shapes = tuple(jax.ShapeDtypeStruct(held.shape, held.dtype) for held in large)
    results = pl.pallas_call(
        settle,
        out_shape=shapes + (jax.ShapeDtypeStruct((2, 2), F32),),
        in_specs=[vmem] * 6 + [smem],
        out_specs=(vmem,) * 6 + (smem,),
        compiler_params=pltpu.CompilerParams(vmem_limit_bytes=VLIM2 * 1024 * 1024),
    )(*large, outs[5])
    return (results[0].T,) + tuple(results[1:5]) + (results[6], results[5])


def solution(mesh):
    placed = (
        P("tok", None),
        P("tok"),
        P("tok", None),
        P("tok", "col"),
        P(None, "col"),
        P("col", None),
        P("tok", "col", None, None),
        P("tok", "col", None, None),
        P("tok", "col", None, None),
        P("tok", "col"),
        P("tok", "col"),
    )
    return jax.shard_map(
        per_device,
        mesh=mesh,
        in_specs=placed,
        out_specs=(
            P("tok", "col"),
            P("tok", "col"),
            P("tok", "col", None, None),
            P("tok", "col", None, None),
            P("tok", "col", None, None),
            P("col", None),
            P("tok", "col", None, None),
        ),
        check_vma=False,
    )
```
